256 devices in a mesh: tm: 64 (over x, z, core), space: 4 (over y).
Axes of the slice: x: 4, y: 4, z: 8, core: 2. Of those that a mesh axis runs over, the one named last changes fastest.
Arguments:
- misfit: bfloat16 [512, 32, 64, 128], P('tm', 'space'), may hold values from -2 to 2
- guess: float32 [64, 32, 64, 128], P('tm', 'space'), may hold values from -4 to 4
- rate: float32 [64, 32, 64, 128], P('tm', 'space'), may hold values from 5e-05 to 1.7
- coeffs: float32 [3, 32, 64, 128], P(None, 'space'), may hold values from -0.25 to 0.25
- control: float32 [32, 64, 128], P('space'), may hold values from -6 to 6
Outputs:
- corrected: float32 [64, 32, 64, 128], P('tm', 'space')
- gradient: float32 [32, 64, 128], P('space')
The draws below stay inside these ranges and needn't reach their ends.
All inputs are finite; a program needn't handle non-finite values.
Results may differ from the reference program's by a relative error of at most 0.0003.
Values sent between devices are 32-bit elements; how exact they have to be, the bound alone decides.
A program may use at most 128 MiB of HBM per device.

```python
import math
import jax
import jax.numpy as jnp
from jax import lax

CELLS_SECOND_AXIS = 64
CELLS_THIRD_AXIS = 128
STEPS = 8
SLABS = 64
CELLS_FIRST_AXIS = 32


def draw_rate(key, part):
    key = jax.random.fold_in(key, 11)
    first, second, third, fourth_part = jax.random.split(key, 4)
    upper = 0.5
    baseline_value = jnp.exp(jax.random.uniform(first, (1, CELLS_FIRST_AXIS, CELLS_SECOND_AXIS, CELLS_THIRD_AXIS), jnp.float32, math.log(0.0001), math.log(upper)))
    slab_jitter = jnp.exp(jax.random.uniform(second, (SLABS, CELLS_FIRST_AXIS, CELLS_SECOND_AXIS, CELLS_THIRD_AXIS), jnp.float32, math.log(0.5), math.log(2.0)))
    chosen = jax.random.randint(third, (3,), 0, SLABS)
    marker_labels = jnp.arange(SLABS, dtype=jnp.int32)[:, None] == chosen[None, :]
    pulse_mask = jnp.any(marker_labels, axis=1).astype(jnp.float32)[:, None, None, None]
    sudden_pulse = jax.random.uniform(fourth_part, (1, CELLS_FIRST_AXIS, CELLS_SECOND_AXIS, CELLS_THIRD_AXIS), jnp.float32, 0.22, 0.69)
    return (baseline_value * slab_jitter + pulse_mask * sudden_pulse).astype(jnp.float32)


def draw_coeffs(key, part):
    key = jax.random.fold_in(key, 7)
    first, second, third = jax.random.split(key, 3)
    sign_value = jnp.where(jax.random.bernoulli(first), 1.0, -1.0).astype(jnp.float32)
    along_first = sign_value * jax.random.uniform(second, (1, CELLS_FIRST_AXIS, CELLS_SECOND_AXIS, CELLS_THIRD_AXIS), jnp.float32, 0.2, 0.25)
    across = jax.random.uniform(third, (2, CELLS_FIRST_AXIS, CELLS_SECOND_AXIS, CELLS_THIRD_AXIS), jnp.float32, -0.25, 0.25)
    return jnp.concatenate([along_first, across], axis=0).astype(jnp.float32)


def shard_levels(rng, dims, pieces, low, largest):
    def one(axis_at, parts):
        draws = jax.random.uniform(jax.random.fold_in(jax.random.fold_in(rng, 6), axis_at), (parts,), jnp.float32, low / len(pieces), largest / len(pieces))
        return jnp.repeat(jnp.exp(draws), dims[axis_at] // parts).reshape((-1,) + (1,) * (len(dims) - axis_at - 1))

    level = one(*pieces[0])
    for cut in pieces[1:]:
        level = level * one(*cut)
    return level


def gaussian(own_key, shape, spread, bound, cuts=(), kind=jnp.bfloat16):
    entries = jax.random.normal(own_key, shape, jnp.float32) * spread
    if len(cuts) > 0:
        entries = shard_levels(own_key, shape, cuts, -0.22, 0.18) * entries
    return jnp.clip(entries, min=-bound, max=bound).astype(kind)


def setup_inputs(seed: int = 0) -> dict:
    seeds = jax.random.split(jax.random.key(seed), 6)
    misfit = gaussian(seeds[0], (SLABS * STEPS, CELLS_FIRST_AXIS, CELLS_SECOND_AXIS, CELLS_THIRD_AXIS), 0.3, 2.0, ((0, 64), (1, 4)))
    guess = gaussian(seeds[1], (SLABS, CELLS_FIRST_AXIS, CELLS_SECOND_AXIS, CELLS_THIRD_AXIS), 0.5, 4.0, ((0, 64), (1, 4)), jnp.float32)
    rate = draw_rate(jax.random.fold_in(seeds[5], 71), 0)
    coeffs = draw_coeffs(jax.random.fold_in(seeds[5], 71), 0)
    control = gaussian(seeds[4], (CELLS_FIRST_AXIS, CELLS_SECOND_AXIS, CELLS_THIRD_AXIS), 1.0, 6.0, ((0, 4),), jnp.float32)
    return dict(misfit=misfit, guess=guess, rate=rate, coeffs=coeffs, control=control)


NU = 0.14
BETA = 0.5


def adjoint_step(field, coeffs, forcing):
    padded = jnp.pad(field, 1)
    beside = padded[2:, 1:-1, 1:-1] + padded[:-2, 1:-1, 1:-1]
    beside = beside + padded[1:-1, 2:, 1:-1] + padded[1:-1, :-2, 1:-1]
    beside = beside + padded[1:-1, 1:-1, 2:] + padded[1:-1, 1:-1, :-2]
    flux_x = jnp.pad(coeffs[0] * field, ((1, 1), (0, 0), (0, 0)))
    flux_y = jnp.pad(coeffs[1] * field, ((0, 0), (1, 1), (0, 0)))
    flux_z = jnp.pad(coeffs[2] * field, ((0, 0), (0, 0), (1, 1)))
    flow = (flux_x[2:] - flux_x[:-2]) + (flux_y[:, 2:] - flux_y[:, :-2]) + (flux_z[:, :, 2:] - flux_z[:, :, :-2])
    return field + NU * (beside - 6.0 * field) + 0.5 * flow + forcing.astype(jnp.float32)


def reference(misfit, guess, rate, coeffs, control):
    slabs_misfit = misfit.reshape(SLABS, STEPS, CELLS_FIRST_AXIS, CELLS_SECOND_AXIS, CELLS_THIRD_AXIS)
    empty = jnp.zeros((1, CELLS_FIRST_AXIS, CELLS_SECOND_AXIS, CELLS_THIRD_AXIS), jnp.float32)
    next_guess = jnp.concatenate([guess[1:], empty], axis=0)

    def first_relax(items):
        start, forcing = items
        field = start
        for j in reversed(range(STEPS)):
            field = adjoint_step(field, coeffs, forcing[j])
        return field

    phi = lax.map(first_relax, (next_guess, slabs_misfit))
    residual = phi - guess
    factor = jnp.exp(-rate)

    def backward(carry, items):
        decay, term = items
        value = decay * carry + term
        return value, value

    unused, correction = lax.scan(backward, jnp.zeros((CELLS_FIRST_AXIS, CELLS_SECOND_AXIS, CELLS_THIRD_AXIS), jnp.float32), (factor, residual), reverse=True)
    corrected = guess + correction
    next_corrected = jnp.concatenate([corrected[1:], empty], axis=0)

    def second_relax(items):
        start, forcing = items
        field = start
        summed = jnp.zeros((CELLS_FIRST_AXIS, CELLS_SECOND_AXIS, CELLS_THIRD_AXIS), jnp.float32)
        for j in reversed(range(1, STEPS)):
            field = adjoint_step(field, coeffs, forcing[j])
            summed = summed + field
        return summed

    partials = lax.map(second_relax, (next_corrected, slabs_misfit))
    total = jnp.sum(partials, axis=0) + jnp.sum(corrected, axis=0)
    gradient = BETA * control + total / (SLABS * STEPS)
    return corrected, gradient
```

```python
import functools
from types import SimpleNamespace

import jax
import jax.numpy as jnp
from jax import lax
from jax.experimental import pallas as pl
from jax.experimental.pallas import tpu as pltpu
from jax.sharding import PartitionSpec as P

NU = 0.14
BETA = 0.5
CENTRE = 1.0 - 6.0 * NU
ROUNDS = (1, 1, 2, 2, 2)
CUT = 99
MESH = pl.DeviceIdType.MESH
F32 = jnp.float32
MAX_MOVES = 64
LOW, HIGH = 0, 1
TIME, SPACE = "tm", "space"


def rolled(value, by, axis):
    return pltpu.roll(value, by % value.shape[axis], axis)


def when(condition, run):
    def body():
        run()

    if condition is None:
        body()
    else:
        pl.when(condition)(body)


class Net:
    def __init__(self, send, recv, here):
        self.send, self.recv, self.here, self.moves = send, recv, here, []

    def move(self, whole, sent=None, got=None):
        return Move(self, whole, sent, got)

    def close(self):
        for move in self.moves:
            move.close()


class Move:
    def __init__(self, net, whole, sent, got):
        self.net, self.whole, self.sent, self.got = net, whole, sent, got
        self.index, self.started, self.arrived = len(net.moves), False, False
        net.moves.append(self)

    def copy(self, src, dst, device):
        return pltpu.make_async_remote_copy(
            src_ref=src, dst_ref=dst, send_sem=self.net.send.at[self.index], recv_sem=self.net.recv.at[self.index],
            device_id=device, device_id_type=MESH,
        )

    def start(self, src, dst, device):
        self.started = True
        when(self.sent, lambda: self.copy(src, dst, device).start())
        return self

    def land(self):
        self.arrived = True
        when(self.got, lambda: self.copy(self.whole, self.whole, self.net.here).wait_recv())

    def close(self):
        if self.started:
            if not self.arrived:
                self.land()
            when(self.sent, lambda: self.copy(self.whole, self.whole, self.net.here).wait_send())


def kernel(cfg, misfit_in, guess_in, rate_in, coeffs_in, e_out, total_out, *scratch):
    buf = SimpleNamespace(**dict(zip(cfg.names, scratch)))
    wf = scratch[len(cfg.names):len(cfg.names) + len(cfg.rounds)]
    mids = scratch[len(cfg.names) + len(cfg.rounds):-4]
    misfit, inputs = scratch[-4], scratch[-3]
    guess, rate, coeffs = buf.guess, buf.rate, buf.coeffs
    fetches = [
        pltpu.make_async_copy(src, dst, inputs.at[i])
        for i, (src, dst) in enumerate(((guess_in, guess), (coeffs_in, coeffs), (misfit_in, misfit), (rate_in, rate)))
    ]
    for fetch in fetches:
        fetch.start()
    steps, rounds, rows, mid, lanes = cfg.steps, cfg.rounds, cfg.rows, cfg.mid, cfg.lanes
    groups, ny = cfg.groups, cfg.ny
    half, members, wide = mid // 2, 2 * rows, steps - 1
    deepest = max(rounds)
    slabs = groups * members

    tm, y = lax.axis_index(TIME), lax.axis_index(SPACE)
    x, spot = tm // members, tm % members
    z, core = spot // 2, spot % 2
    base = x * members
    has_low, has_high = y > 0, y < ny - 1
    has_next, has_before = tm < slabs - 1, tm > 0
    below, above, sibling = (tm, y - 1), (tm, y + 1), (base + spot + 1 - 2 * core, y)

    net = Net(scratch[-2], scratch[-1], (tm, y))
    ax, bx, ay, by, az, bz = buf.ax, buf.bx, buf.ay, buf.by, buf.az, buf.bz
    mine = pl.ds(pl.multiple_of(core * half, half), half)
    other = pl.ds(pl.multiple_of((1 - core) * half, half), half)
    rows_own, rows_low, rows_high = pl.ds(wide, rows), pl.ds(0, wide), pl.ds(wide + rows, wide)

    barrier = pltpu.get_barrier_semaphore()

    def greet(device):
        pl.semaphore_signal(barrier, inc=1, device_id=device, device_id_type=MESH)

    def greet_member(i, _):
        greet((base + (spot + i) % members, y))
        return 0

    lax.fori_loop(1, members, greet_member, 0)
    for i in range(1, groups):
        greet(((x + i) % groups * members + spot, y))
    when(has_low, lambda: greet(below))
    when(has_high, lambda: greet(above))
    for exists, there in ((has_next, tm + 1), (has_before, tm - 1)):
        when(exists, lambda: greet((there, y)))
        when(exists & has_low, lambda: greet((there, y - 1)))
        when(exists & has_high, lambda: greet((there, y + 1)))
    sides = has_low.astype(jnp.int32) + has_high.astype(jnp.int32)
    ends = has_next.astype(jnp.int32) + has_before.astype(jnp.int32)

    for fetch in fetches:
        fetch.wait()
    for r, n in enumerate(rounds):
        for s in range(n - 1):
            k, turn, width = cfg.forcing_at[(r, s)], sum(rounds[:r]) + s, n - 1 - s
            for i in range(width):
                buf.f_send[LOW, k + i] = misfit[steps - 1 - turn, rows - width + i].astype(F32)
                buf.f_send[HIGH, k + i] = misfit[steps - 1 - turn, i].astype(F32)

    pl.semaphore_wait(barrier, members - 1 + groups - 1 + sides + ends + sides * ends)
    if cfg.cut == 0:
        return net.close()

    first = rounds[0]
    start = net.move(wf[0].at[pl.ds(first, rows)], has_before, has_next)
    start.start(guess, wf[0].at[pl.ds(first, rows)], (tm - 1, y))

    def up_down(low, high, whole_low, whole_high):
        up = net.move(whole_low, has_high, has_low)
        down = net.move(whole_high, has_low, has_high)
        up.start(low[0], low[1], above)
        down.start(high[0], high[1], below)
        return up, down

    lows, highs = wf[0].at[pl.ds(0, first)], wf[0].at[pl.ds(first + rows, first)]
    start_up = net.move(lows, has_before & has_high, has_next & has_low)
    start_up.start(guess.at[pl.ds(rows - first, first)], lows, (tm - 1, y + 1))
    start_down = net.move(highs, has_before & has_low, has_next & has_high)
    start_down.start(guess.at[pl.ds(0, first)], highs, (tm - 1, y - 1))
    start_faces = (start_up, start_down)

    def both_ends(src, at_low, at_high, dst):
        return up_down((src.at[at_high], dst.at[LOW]), (src.at[at_low], dst.at[HIGH]), dst.at[LOW], dst.at[HIGH])

    def ends(src, width, dst, at=0):
        low, high = pl.ds(at, width), pl.ds(rows - at - width, width)
        to_low, to_high = pl.ds(deepest - at - width, width), pl.ds(at, width)
        up, down = dst.at[LOW, to_low], dst.at[HIGH, to_high]
        return up_down((src.at[high], up), (src.at[low], down), up, down)

    beside = ends(coeffs.at[0], 1, buf.cx)
    further = []
    if deepest > 1:
        count = deepest - 1
        further.append(ends(coeffs.at[0], count, buf.cx, 1))
        for i in range(2):
            low, high = buf.cyz.at[LOW, i], buf.cyz.at[HIGH, i]
            further.append(up_down(
                (coeffs.at[1 + i, pl.ds(rows - count, count)], low), (coeffs.at[1 + i, pl.ds(0, count)], high), low, high))
        low, high = buf.f_halo.at[LOW], buf.f_halo.at[HIGH]
        further.append(up_down((buf.f_send.at[LOW], low), (buf.f_send.at[HIGH], high), low, high))

    def transpose(src, dst):
        move = net.move(dst.at[pl.ds(0, members - 1)])

        def send(i, _):
            to = (spot + i) % members
            part = src.at[to // 2, pl.ds(pl.multiple_of(to % 2 * half, half), half)]
            move.start(part, dst.at[spot], (base + to, y))
            return 0

        lax.fori_loop(1, members, send, 0)
        dst[spot] = src[z, mine]
        return move

    def across(src, dst):
        move = net.move(dst.at[pl.ds(0, groups - 1)])
        for i in range(1, groups):
            move.start(src, dst.at[x], ((x + i) % groups * members + spot, y))
        dst[x] = src[...]
        return move

    def along(source, target, whole):
        move = net.move(whole)

        def send(i, _):
            to = (z + i) % rows
            move.start(source(to), target, (base + 2 * to + core, y))
            return 0

        lax.fori_loop(1, rows, send, 0)
        return move

    def factors_x(row, c):
        ax[row] = NU + 0.5 * c
        bx[row] = NU - 0.5 * c

    def factors_yz(row, cy, cz):
        place = lax.broadcasted_iota(jnp.int32, (mid, lanes), 0)
        ay[row] = jnp.where(place == 0, 0.0, NU + 0.5 * cy)
        by[row] = jnp.where(place == mid - 1, 0.0, NU - 0.5 * cy)
        place = lax.broadcasted_iota(jnp.int32, (mid, lanes), 1)
        az[row] = jnp.where(place == 0, 0.0, NU + 0.5 * cz)
        bz[row] = jnp.where(place == lanes - 1, 0.0, NU - 0.5 * cz)

    def each(start, stop, run, unroll=1):
        def one(i, _):
            run(i)
            return 0

        if stop > start:
            lax.fori_loop(start, stop, one, 0, unroll=unroll if (stop - start) % unroll == 0 else 1)

    def own_factors(i):
        factors_x(wide + i, coeffs[0, i])
        factors_yz(wide + i, coeffs[1, i], coeffs[2, i])

    each(0, rows, own_factors, 2)

    def clear(ref, start, count):
        def one(i):
            ref[i] = jnp.zeros((mid, lanes), F32)

        each(start, start + count, one)

    halos = [(ref, n) for ref, n in zip(wf[1:], rounds[1:])] + [(ref, deepest - 1) for ref in mids]
    halos += [(buf.e, wide), (buf.e1, wide), (buf.e2, wide)]

    @pl.when(jnp.logical_not(has_low))
    def _():
        clear(bx, 0, wide)
        for ref, n in halos:
            clear(ref, 0, n)

    @pl.when(jnp.logical_not(has_high))
    def _():
        clear(ax, wide + rows, wide)
        for ref, n in halos:
            clear(ref, n + rows, n)

    when(jnp.logical_not(has_next & has_low), lambda: clear(wf[0], 0, first))
    when(jnp.logical_not(has_next & has_high), lambda: clear(wf[0], first + rows, first))
    when(jnp.logical_not(has_next), lambda: clear(wf[0], first, rows))

    def stepped(src, at, row):
        w = src[at]
        place = row + wide
        value = CENTRE * w
        value = value + (ax[place + 1] * src[at + 1] + bx[place - 1] * src[at - 1])
        value = value + (rolled(ay[place] * w, -1, 0) + rolled(by[place] * w, 1, 0))
        return value + (rolled(az[place] * w, -1, 1) + rolled(bz[place] * w, 1, 1))

    def relax_row(r, s, row, side=None):
        n = rounds[r]
        turn = sum(rounds[:r]) + s
        src, shift = (wf[r], n) if s == 0 else (mids[s - 1], deepest - 1)
        if side is None:
            forcing = misfit[steps - 1 - turn, row].astype(F32)
        elif side == LOW:
            forcing = buf.f_halo[LOW, cfg.forcing_at[(r, s)] + (n - 1 - s) + row]
        else:
            forcing = buf.f_halo[HIGH, cfg.forcing_at[(r, s)] + row - rows]
        value = stepped(src, row + shift, row) + forcing
        if s < n - 1:
            mids[s][row + deepest - 1] = value
        elif r < len(rounds) - 1:
            wf[r + 1][row + rounds[r + 1]] = value
        if side is None:
            if turn == 0:
                buf.d[row] = guess[row] + value
            elif turn < steps - 1:
                buf.d[row] = buf.d[row] + value
            else:
                buf.res[row] = value - guess[row]

    def inner(r):
        for s in range(rounds[r]):
            each(s + 1, rows - 1 - s, lambda row: relax_row(r, s, row), 2)

    def outer(r, side):
        for s in range(rounds[r]):
            reach = rounds[r] - 1 - s
            if side == LOW:
                when(has_low, lambda: [relax_row(r, s, row, LOW) for row in range(-reach, 0)])
                for row in range(s + 1):
                    relax_row(r, s, row)
            else:
                when(has_high, lambda: [relax_row(r, s, row, HIGH) for row in range(rows, rows + reach)])
                for row in range(rows - 1 - s, rows):
                    relax_row(r, s, row)

    def beside_factors(side):
        if side == HIGH:
            factors_x(wide + rows, buf.cx[side, 0])
        else:
            factors_x(wide - 1, buf.cx[side, deepest - 1])

    def further_factors(side):
        at = wide + rows if side == HIGH else wide - deepest
        each(0, deepest, lambda i: factors_x(at + i, buf.cx[side, i]))
        at = wide + rows if side == HIGH else wide - deepest + 1
        each(0, deepest - 1, lambda i: factors_yz(at + i, buf.cyz[side, 0, i], buf.cyz[side, 1, i]))

    def decays():
        rates.land()
        last = members - 1
        factor = jnp.exp(-buf.rates[last])
        buf.decay[last] = factor
        buf.upto[last] = factor

        def one(i, carry):
            upto, summed = carry
            k = last - i
            factor = jnp.exp(-buf.rates[k])
            upto = factor * upto
            buf.decay[k] = factor
            buf.upto[k] = upto
            return upto, summed + jnp.where((k > 0) | (x > 0), upto, 0.0)

        buf.fx_send[0], buf.fx_send[1] = lax.fori_loop(1, members, one, (factor, factor))
        return across(buf.fx_send, buf.fx)

    start.land()
    if cfg.cut == 20:
        return net.close()
    faces = start_faces
    for r in range(len(rounds)):
        inner(r)
        if r == len(rounds) - 2:
            group_decay = decays()
        if r < len(rounds) - 1:
            n, ref = rounds[r + 1], wf[r + 1]
            low, high = ref.at[pl.ds(0, n)], ref.at[pl.ds(n + rows, n)]
            coming = net.move(low, has_high, has_low), net.move(high, has_low, has_high)
        for side, exists in ((LOW, has_low), (HIGH, has_high)):
            if r == 0:
                beside[side].land()
                when(exists, lambda: beside_factors(side))
            if rounds[r] > 1 and max((1,) + rounds[:r]) == 1:
                for pair in further:
                    pair[side].land()
                when(exists, lambda: further_factors(side))
            faces[side].land()
            outer(r, side)
            if r < len(rounds) - 1:
                if side == LOW:
                    coming[HIGH].start(ref.at[pl.ds(n, n)], high, below)
                else:
                    coming[LOW].start(ref.at[pl.ds(rows, n)], low, above)
        if cfg.cut == 1 + r:
            return net.close()
        if r == 0:
            rates = transpose(rate, buf.rates)
        if r < len(rounds) - 1:
            faces = coming

    terms = transpose(buf.res, buf.terms)
    pair = net.move(buf.d_pair).start(buf.d.at[:, other], buf.d_pair, sibling)
    far = up_down(
        (coeffs.at[:, pl.ds(rows - wide, wide), mine], buf.far.at[LOW, :, :, mine]),
        (coeffs.at[:, pl.ds(0, wide), mine], buf.far.at[HIGH, :, :, mine]),
        buf.far.at[LOW, :, :, mine], buf.far.at[HIGH, :, :, mine],
    )

    terms.land()
    if cfg.cut == 10:
        return net.close()
    last = members - 1
    value = buf.terms[last]
    buf.local[last] = value

    def solve(i, carry):
        value, summed = carry
        k = last - i
        value = buf.decay[k] * value + buf.terms[k]
        buf.local[k] = value
        return value, summed + jnp.where((k > 0) | (x > 0), value, 0.0)

    buf.rx_send[0], buf.rx_send[1] = lax.fori_loop(1, members, solve, (value, value))
    group_result = across(buf.rx_send, buf.rx)

    pair.land()

    def pair_sum(i):
        buf.d_chip[i] = buf.d[i, mine] + buf.d_pair[i]

    each(0, rows, pair_sum)
    ring = along(lambda to: buf.d_chip.at[to], buf.d_ring.at[z], buf.d_ring.at[pl.ds(0, rows - 1)])
    buf.d_ring[z] = buf.d_chip[z]

    far_pair = []
    for side, exists in ((LOW, has_low), (HIGH, has_high)):
        far[side].land()
        part = buf.far.at[side, :, :, mine]
        far_pair.append(net.move(part, exists, exists).start(part, part, sibling))

    group_decay.land()
    group_result.land()
    if cfg.cut == 11:
        return net.close()
    carry = jnp.zeros((half, lanes), F32)
    e_sum = carry
    for group in reversed(range(groups)):
        buf.carry[group] = carry
        e_sum = e_sum + (buf.rx[group, 1] + buf.fx[group, 1] * carry)
        carry = buf.rx[group, 0] + buf.fx[group, 0] * carry
    e, t = buf.e, buf.t
    e[wide + z, mine] = e_sum
    e_mine = e.at[wide + z, mine]
    e_ring = along(lambda to: e_mine, e_mine, e.at[pl.ds(wide, rows - 1), mine])
    buf.t_own[...] = e_sum + carry

    carry = buf.carry[x]

    def finish(k):
        buf.back[k] = buf.local[k] + buf.upto[k] * carry

    each(0, members, finish)
    back = net.move(buf.back.at[pl.ds(0, members - 1)])

    def send_back(i):
        to = (spot + i) % members
        back.start(buf.back.at[to], buf.e_own.at[z, mine], (base + to, y))

    each(1, members, send_back)
    buf.e_own[z, mine] = buf.back[spot]

    e_ring.land()
    if cfg.cut == 12:
        return net.close()
    e_faces = up_down(
        (e.at[pl.ds(rows, wide), mine], e.at[rows_low, mine]), (e.at[pl.ds(wide, wide), mine], e.at[rows_high, mine]),
        e.at[rows_low, mine], e.at[rows_high, mine],
    )
    e_pair = net.move(e.at[rows_own, mine]).start(e.at[rows_own, mine], e.at[rows_own, mine], sibling)

    ring.land()
    buf.dx_send[...] = lax.fori_loop(1, rows, lambda i, s: s + buf.d_ring[i], buf.d_ring[0])
    d_across = across(buf.dx_send, buf.dx)

    def far_factors(side):
        def one(i):
            row = wide + rows + i if side == HIGH else i
            factors_x(row, buf.far[side, 0, i])
            factors_yz(row, buf.far[side, 1, i], buf.far[side, 2, i])

        each(0, wide, one)

    for side, exists in ((LOW, has_low), (HIGH, has_high)):
        far_pair[side].land()
        when(exists, lambda: far_factors(side))

    e_pairs = [e_pair]
    for side, exists, where in ((LOW, has_low, rows_low), (HIGH, has_high, rows_high)):
        e_faces[side].land()
        part = e.at[where, mine]
        e_pairs.append(net.move(part, exists, exists).start(part, part, sibling))

    d_across.land()
    t_mine = buf.t_own[...]
    for group in range(groups):
        t_mine = t_mine + buf.dx[group]
    t[z, mine] = t_mine
    t_ring = along(lambda to: t.at[z, mine], t.at[z, mine], t.at[pl.ds(0, rows - 1), mine])

    for pair in e_pairs:
        pair.land()
    if cfg.cut == 13:
        return net.close()

    for s in range(steps - 1):
        if s == min(2, steps - 2):
            t_ring.land()
            t_pair = net.move(t.at[:, mine]).start(t.at[:, mine], t.at[:, mine], sibling)
        src = (e, buf.e1, buf.e2)[0 if s == 0 else 1 + (s - 1) % 2]
        dst = (buf.e1, buf.e2)[s % 2]
        reach = steps - 2 - s

        def halo_row(row):
            dst[row + wide] = stepped(src, row + wide, row)

        def own_row(row):
            value = stepped(src, row + wide, row)
            dst[row + wide] = value
            buf.sum[row] = value if s == 0 else buf.sum[row] + value

        when(has_low, lambda: each(-reach, 0, halo_row, 2))
        when(has_high, lambda: each(rows, rows + reach, halo_row, 2))
        each(0, rows, own_row, 2)

    back.land()
    e_out[...] = buf.e_own[...]
    t_pair.land()
    total_out[...] = t[...] + buf.sum[...]
    net.close()


def exchange(mesh, misfit, guess, rate, coeffs, rounds, cut):
    steps, rows, mid, lanes = misfit.shape
    members, half, wide = 2 * rows, mid // 2, steps - 1
    ny = mesh.shape[SPACE]
    groups = mesh.shape[TIME] // members
    deepest = max(rounds)
    forcing_at, count = {}, 0
    for r, n in enumerate(rounds):
        for s in range(n - 1):
            forcing_at[(r, s)] = count
            count += n - 1 - s
    plane, part = (mid, lanes), (half, lanes)
    field, long, slots = (rows,) + plane, (rows + 2 * wide,) + plane, (members,) + part
    shapes = dict(
        guess=field, rate=field, coeffs=(3,) + field,
        cx=(2, deepest) + plane, cyz=(2, 2, max(deepest - 1, 1)) + plane,
        f_send=(2, max(count, 1)) + plane, f_halo=(2, max(count, 1)) + plane,
        rates=slots, decay=slots, upto=slots, fx_send=(2,) + part, fx=(groups, 2) + part,
        res=field, d=field, d_pair=(rows,) + part, d_chip=(rows,) + part, d_ring=(rows,) + part,
        dx_send=part, dx=(groups,) + part, t_own=part,
        terms=slots, local=slots, rx_send=(2,) + part, rx=(groups, 2) + part,
        carry=(groups,) + part, back=slots, e_own=field, t=field, sum=field, far=(2, 3, wide) + plane,
        ax=long, bx=long, ay=long, by=long, az=long, bz=long, e=long, e1=long, e2=long,
    )
    extra = [(rows + 2 * n,) + plane for n in rounds] + [(rows + 2 * (deepest - 1),) + plane] * (deepest - 1)
    cfg = SimpleNamespace(
        names=list(shapes), steps=steps, rounds=rounds, rows=rows, mid=mid, lanes=lanes, groups=groups, ny=ny,
        forcing_at=forcing_at, cut=cut,
    )
    in_vmem, in_hbm = pl.BlockSpec(memory_space=pltpu.VMEM), pl.BlockSpec(memory_space=pltpu.HBM)
    return pl.pallas_call(
        functools.partial(kernel, cfg),
        out_shape=[jax.ShapeDtypeStruct(field, F32)] * 2,
        in_specs=[in_hbm] * 4,
        out_specs=[in_vmem] * 2,
        scratch_shapes=[pltpu.VMEM(shape, F32) for shape in list(shapes.values()) + extra]
        + [pltpu.VMEM(misfit.shape, misfit.dtype), pltpu.SemaphoreType.DMA((4,))]
        + [pltpu.SemaphoreType.DMA((MAX_MOVES,))] * 2,
        compiler_params=pltpu.CompilerParams(
            collective_id=0, has_side_effects=True, vmem_limit_bytes=60 * 1024 * 1024),
        name="cycle",
    )(misfit, guess, rate, coeffs)


def on_device(mesh, rounds, cut, misfit, guess, rate, coeffs, control):
    correction, total = exchange(mesh, misfit, guess[0], rate[0], coeffs, rounds, cut)
    corrected = guess[0] + correction
    gradient = BETA * control + total / (mesh.shape[TIME] * misfit.shape[0])
    return corrected[None], gradient


def solution(mesh, rounds=ROUNDS, cut=CUT):
    slab, block = P(TIME, SPACE, None, None), P(SPACE, None, None)
    return jax.shard_map(
        functools.partial(on_device, mesh, rounds, cut),
        mesh=mesh,
        in_specs=(slab, slab, slab, P(None, SPACE, None, None), block),
        out_specs=(slab, block),
        check_vma=False,
    )
```

```python
import functools
from types import SimpleNamespace

import jax
import jax.numpy as jnp
from jax import lax
from jax.experimental import pallas as pl
from jax.experimental.pallas import tpu as pltpu
from jax.sharding import PartitionSpec as P

NU = 0.14
BETA = 0.5
CENTRE = 1.0 - 6.0 * NU
ROUNDS = (1, 2, 2, 3)
MESH = pl.DeviceIdType.MESH
F32 = jnp.float32
MAX_MOVES = 64
LOW, HIGH = 0, 1
TIME, SPACE = "tm", "space"


def rolled(value, by, axis):
    return pltpu.roll(value, by % value.shape[axis], axis)


def when(condition, run):
    def body():
        run()

    if condition is None:
        body()
    else:
        pl.when(condition)(body)


class Net:
    def __init__(self, send, recv, here):
        self.send, self.recv, self.here, self.moves = send, recv, here, []

    def move(self, whole, sent=None, got=None):
        return Move(self, whole, sent, got)

    def close(self):
        for move in self.moves:
            move.close()


class Move:
    def __init__(self, net, whole, sent, got):
        self.net, self.whole, self.sent, self.got = net, whole, sent, got
        self.index, self.started, self.arrived = len(net.moves), False, False
        net.moves.append(self)

    def copy(self, src, dst, device):
        return pltpu.make_async_remote_copy(
            src_ref=src, dst_ref=dst, send_sem=self.net.send.at[self.index], recv_sem=self.net.recv.at[self.index],
            device_id=device, device_id_type=MESH,
        )

    def start(self, src, dst, device):
        self.started = True
        when(self.sent, lambda: self.copy(src, dst, device).start())
        return self

    def land(self):
        self.arrived = True
        when(self.got, lambda: self.copy(self.whole, self.whole, self.net.here).wait_recv())

    def close(self):
        if self.started:
            if not self.arrived:
                self.land()
            when(self.sent, lambda: self.copy(self.whole, self.whole, self.net.here).wait_send())


def kernel(cfg, misfit_in, guess_in, rate_in, coeffs_in, control_in, corrected_out, gradient_out, *scratch):
    buf = SimpleNamespace(**dict(zip(cfg.names, scratch)))
    wf = scratch[len(cfg.names):len(cfg.names) + len(cfg.rounds)]
    mids = scratch[len(cfg.names) + len(cfg.rounds):-4]
    misfit, inputs = scratch[-4], scratch[-3]
    guess, rate, coeffs = buf.guess, buf.rate, buf.coeffs
    fetches = [
        pltpu.make_async_copy(src, dst, inputs.at[i])
        for i, (src, dst) in enumerate(((guess_in, guess), (coeffs_in, coeffs), (misfit_in, misfit), (rate_in, rate), (control_in, buf.control)))
    ]
    for fetch in fetches:
        fetch.start()
    steps, rounds, rows, mid, lanes = cfg.steps, cfg.rounds, cfg.rows, cfg.mid, cfg.lanes
    groups, ny = cfg.groups, cfg.ny
    half, members, wide = mid // 2, 2 * rows, steps - 1
    deepest = max(rounds)
    slabs = groups * members

    tm, y = lax.axis_index(TIME), lax.axis_index(SPACE)
    x, spot = tm // members, tm % members
    z, core = spot // 2, spot % 2
    base = x * members
    has_low, has_high = y > 0, y < ny - 1
    has_next, has_before = tm < slabs - 1, tm > 0
    below, above, sibling = (tm, y - 1), (tm, y + 1), (base + spot + 1 - 2 * core, y)

    net = Net(scratch[-2], scratch[-1], (tm, y))
    ax, bx, ay, by, az, bz = buf.ax, buf.bx, buf.ay, buf.by, buf.az, buf.bz
    mine = pl.ds(pl.multiple_of(core * half, half), half)
    other = pl.ds(pl.multiple_of((1 - core) * half, half), half)
    rows_own, rows_low, rows_high = pl.ds(wide, rows), pl.ds(0, wide), pl.ds(wide + rows, wide)

    barrier = pltpu.get_barrier_semaphore()

    def greet(device):
        pl.semaphore_signal(barrier, inc=1, device_id=device, device_id_type=MESH)

    def greet_member(i, _):
        greet((base + (spot + i) % members, y))
        return 0

    when(has_low, lambda: greet(below))
    when(has_high, lambda: greet(above))
    for exists, there in ((has_next, tm + 1), (has_before, tm - 1)):
        when(exists, lambda: greet((there, y)))
        when(exists & has_low, lambda: greet((there, y - 1)))
        when(exists & has_high, lambda: greet((there, y + 1)))
    lax.fori_loop(1, members, greet_member, 0)
    for i in range(1, groups):
        greet(((x + i) % groups * members + spot, y))
    sides = has_low.astype(jnp.int32) + has_high.astype(jnp.int32)
    ends = has_next.astype(jnp.int32) + has_before.astype(jnp.int32)

    for fetch in fetches:
        fetch.wait()
    for r, n in enumerate(rounds):
        for s in range(n - 1):
            k, turn, width = cfg.forcing_at[(r, s)], sum(rounds[:r]) + s, n - 1 - s
            for i in range(width):
                buf.f_send[LOW, k + i] = misfit[steps - 1 - turn, rows - width + i].astype(F32)
                buf.f_send[HIGH, k + i] = misfit[steps - 1 - turn, i].astype(F32)

    pl.semaphore_wait(barrier, members - 1 + groups - 1 + sides + ends + sides * ends)

    first = rounds[0]
    start = net.move(wf[0].at[pl.ds(first, rows)], has_before, has_next)
    start.start(guess, wf[0].at[pl.ds(first, rows)], (tm - 1, y))

    def up_down(low, high, whole_low, whole_high):
        up = net.move(whole_low, has_high, has_low)
        down = net.move(whole_high, has_low, has_high)
        up.start(low[0], low[1], above)
        down.start(high[0], high[1], below)
        return up, down

    lows, highs = wf[0].at[pl.ds(0, first)], wf[0].at[pl.ds(first + rows, first)]
    start_up = net.move(lows, has_before & has_high, has_next & has_low)
    start_up.start(guess.at[pl.ds(rows - first, first)], lows, (tm - 1, y + 1))
    start_down = net.move(highs, has_before & has_low, has_next & has_high)
    start_down.start(guess.at[pl.ds(0, first)], highs, (tm - 1, y - 1))
    start_faces = (start_up, start_down)

    def both_ends(src, at_low, at_high, dst):
        return up_down((src.at[at_high], dst.at[LOW]), (src.at[at_low], dst.at[HIGH]), dst.at[LOW], dst.at[HIGH])

    def ends(src, at, width, low_halo, high_halo, depth):
        up, down = low_halo.at[pl.ds(depth - at - width, width)], high_halo.at[pl.ds(at, width)]
        return up_down((src.at[pl.ds(rows - at - width, width)], up), (src.at[pl.ds(at, width)], down), up, down)

    def reach_of(r):
        before = max((0,) + rounds[:r])
        after = max(before, rounds[r])
        return before, after, max(before - 1, 0), after - 1

    def near_stage(r):
        before, after, yz_before, yz_after = reach_of(r)
        moves = []
        if after > before:
            moves.append(ends(coeffs.at[0], before, after - before, buf.cx.at[LOW], buf.cx.at[HIGH], deepest))
        if yz_after > yz_before:
            for i in range(2):
                moves.append(ends(coeffs.at[1 + i], yz_before, yz_after - yz_before, buf.cyz.at[LOW, i], buf.cyz.at[HIGH, i],
                                  deepest - 1))
        n = rounds[r]
        if n > 1:
            part = pl.ds(cfg.forcing_at[(r, 0)], n * (n - 1) // 2)
            low, high = buf.f_halo.at[LOW, part], buf.f_halo.at[HIGH, part]
            moves.append(up_down((buf.f_send.at[LOW, part], low), (buf.f_send.at[HIGH, part], high), low, high))
        return moves

    near = [near_stage(r) for r in range(min(2, len(rounds)))]

    def transpose(src, dst):
        move = net.move(dst.at[pl.ds(0, members - 1)])

        def send(i, _):
            to = (spot + i) % members
            part = src.at[to // 2, pl.ds(pl.multiple_of(to % 2 * half, half), half)]
            move.start(part, dst.at[spot], (base + to, y))
            return 0

        lax.fori_loop(1, members, send, 0)
        dst[spot] = src[z, mine]
        return move

    def across(src, dst):
        move = net.move(dst.at[pl.ds(0, groups - 1)])
        for i in range(1, groups):
            move.start(src, dst.at[x], ((x + i) % groups * members + spot, y))
        dst[x] = src[...]
        return move

    def along(source, target, whole):
        move = net.move(whole)

        def send(i, _):
            to = (z + i) % rows
            move.start(source(to), target, (base + 2 * to + core, y))
            return 0

        lax.fori_loop(1, rows, send, 0)
        return move

    def factors_x(row, c):
        ax[row] = NU + 0.5 * c
        bx[row] = NU - 0.5 * c

    def factors_yz(row, cy, cz):
        place = lax.broadcasted_iota(jnp.int32, (mid, lanes), 0)
        ay[row] = jnp.where(place == 0, 0.0, NU + 0.5 * cy)
        by[row] = jnp.where(place == mid - 1, 0.0, NU - 0.5 * cy)
        place = lax.broadcasted_iota(jnp.int32, (mid, lanes), 1)
        az[row] = jnp.where(place == 0, 0.0, NU + 0.5 * cz)
        bz[row] = jnp.where(place == lanes - 1, 0.0, NU - 0.5 * cz)

    def each(start, stop, run, unroll=1):
        def one(i, _):
            run(i)
            return 0

        if stop > start:
            lax.fori_loop(start, stop, one, 0, unroll=min(unroll, stop - start))

    def own_factors(i):
        factors_x(wide + i, coeffs[0, i])
        factors_yz(wide + i, coeffs[1, i], coeffs[2, i])

    each(0, rows, own_factors, 4)

    def clear(ref, start, count):
        def one(i):
            ref[i] = jnp.zeros((mid, lanes), F32)

        each(start, start + count, one)

    halos = [(ref, n) for ref, n in zip(wf[1:], rounds[1:])] + [(buf.e, wide), (buf.e1, wide), (buf.e2, wide)]

    @pl.when(jnp.logical_not(has_low))
    def _():
        clear(bx, 0, wide)
        for ref, n in halos:
            clear(ref, 0, n)

    @pl.when(jnp.logical_not(has_high))
    def _():
        clear(ax, wide + rows, wide)
        for ref, n in halos:
            clear(ref, n + rows, n)

    when(jnp.logical_not(has_next & has_low), lambda: clear(wf[0], 0, first))
    when(jnp.logical_not(has_next & has_high), lambda: clear(wf[0], first + rows, first))
    when(jnp.logical_not(has_next), lambda: clear(wf[0], first, rows))

    def stepped(src, at, row):
        w = src[at]
        place = row + wide
        value = CENTRE * w
        value = value + (ax[place + 1] * src[at + 1] + bx[place - 1] * src[at - 1])
        value = value + (rolled(ay[place] * w, -1, 0) + rolled(by[place] * w, 1, 0))
        return value + (rolled(az[place] * w, -1, 1) + rolled(bz[place] * w, 1, 1))

    def relax_row(r, s, row, side=None):
        n = rounds[r]
        turn = sum(rounds[:r]) + s
        src, shift = (wf[r], n) if s == 0 else (mids[s - 1], deepest - 1)
        if side is None:
            forcing = misfit[steps - 1 - turn, row].astype(F32)
        elif side == LOW:
            forcing = buf.f_halo[LOW, cfg.forcing_at[(r, s)] + (n - 1 - s) + row]
        else:
            forcing = buf.f_halo[HIGH, cfg.forcing_at[(r, s)] + row - rows]
        value = stepped(src, row + shift, row) + forcing
        if side is not None:
            value = jnp.where(has_low if side == LOW else has_high, value, 0.0)
        if s < n - 1:
            mids[s][row + deepest - 1] = value
        elif r < len(rounds) - 1:
            wf[r + 1][row + rounds[r + 1]] = value
        if side is None:
            if turn == 0:
                buf.d[row] = guess[row] + value
            elif turn < steps - 1:
                buf.d[row] = buf.d[row] + value
            else:
                buf.res[row] = value - guess[row]

    def inner(r):
        for s in range(rounds[r]):
            each(s + 1, rows - 1 - s, lambda row: relax_row(r, s, row), rows)

    def outer(r):
        for s in range(rounds[r]):
            reach = rounds[r] - 1 - s
            for i in range(reach):
                relax_row(r, s, -1 - i, LOW)
                relax_row(r, s, rows + i, HIGH)
            for i in range(s + 1):
                relax_row(r, s, i)
                relax_row(r, s, rows - 1 - i)

    def near_factors(r, side):
        before, after, yz_before, yz_after = reach_of(r)
        for k in range(before, after):
            if side == HIGH:
                factors_x(wide + rows + k, buf.cx[HIGH, k])
            else:
                factors_x(wide - 1 - k, buf.cx[LOW, deepest - 1 - k])
        for k in range(yz_before, yz_after):
            if side == HIGH:
                factors_yz(wide + rows + k, buf.cyz[HIGH, 0, k], buf.cyz[HIGH, 1, k])
            else:
                factors_yz(wide - 1 - k, buf.cyz[LOW, 0, deepest - 2 - k], buf.cyz[LOW, 1, deepest - 2 - k])

    def decays():
        rates.land()
        last = members - 1
        factor = jnp.exp(-buf.rates[last])
        buf.decay[last] = factor
        buf.upto[last] = factor

        def one(i, carry):
            upto, summed = carry
            k = last - i
            factor = jnp.exp(-buf.rates[k])
            upto = factor * upto
            buf.decay[k] = factor
            buf.upto[k] = upto
            return upto, summed + jnp.where((k > 0) | (x > 0), upto, 0.0)

        buf.fx_send[0], buf.fx_send[1] = lax.fori_loop(1, members, one, (factor, factor), unroll=3)
        return across(buf.fx_send, buf.fx)

    start.land()
    faces = start_faces
    for r in range(len(rounds)):
        inner(r)
        if r < len(rounds) - 1:
            n, ref = rounds[r + 1], wf[r + 1]
            low, high = ref.at[pl.ds(0, n)], ref.at[pl.ds(n + rows, n)]
            coming = net.move(low, has_high, has_low), net.move(high, has_low, has_high)
        for side, exists in ((LOW, has_low), (HIGH, has_high)):
            for pair in near[r]:
                pair[side].land()
            if near[r]:
                when(exists, lambda: near_factors(r, side))
            faces[side].land()
        outer(r)
        if r < len(rounds) - 1:
            coming[HIGH].start(ref.at[pl.ds(n, n)], high, below)
            coming[LOW].start(ref.at[pl.ds(rows, n)], low, above)
            if r + 2 < len(rounds):
                near.append(near_stage(r + 2))
        if r == 0:
            rates = transpose(rate, buf.rates)
        if r < len(rounds) - 1:
            faces = coming

    terms = transpose(buf.res, buf.terms)
    pair = net.move(buf.d_pair).start(buf.d.at[:, other], buf.d_pair, sibling)
    far = up_down(
        (coeffs.at[:, pl.ds(rows - wide, wide), mine], buf.far.at[LOW, :, :, mine]),
        (coeffs.at[:, pl.ds(0, wide), mine], buf.far.at[HIGH, :, :, mine]),
        buf.far.at[LOW, :, :, mine], buf.far.at[HIGH, :, :, mine],
    )

    group_decay = decays()

    terms.land()
    last = members - 1
    value = buf.terms[last]
    buf.local[last] = value

    def solve(i, carry):
        value, summed = carry
        k = last - i
        value = buf.decay[k] * value + buf.terms[k]
        buf.local[k] = value
        return value, summed + jnp.where((k > 0) | (x > 0), value, 0.0)

    buf.rx_send[0], buf.rx_send[1] = lax.fori_loop(1, members, solve, (value, value), unroll=5)
    group_result = across(buf.rx_send, buf.rx)

    pair.land()

    def pair_sum(i):
        buf.d_chip[i] = buf.d[i, mine] + buf.d_pair[i]

    each(0, rows, pair_sum, rows)
    ring = along(lambda to: buf.d_chip.at[to], buf.d_ring.at[z], buf.d_ring.at[pl.ds(0, rows - 1)])
    buf.d_ring[z] = buf.d_chip[z]

    far_pair = []
    for side, exists in ((LOW, has_low), (HIGH, has_high)):
        far[side].land()
        part = buf.far.at[side, :, :, mine]
        far_pair.append(net.move(part, exists, exists).start(part, part, sibling))

    group_decay.land()
    group_result.land()
    carry = jnp.zeros((half, lanes), F32)
    e_sum = carry
    for group in reversed(range(groups)):
        buf.carry[group] = carry
        e_sum = e_sum + (buf.rx[group, 1] + buf.fx[group, 1] * carry)
        carry = buf.rx[group, 0] + buf.fx[group, 0] * carry
    e, t = buf.e, buf.t
    e[wide + z, mine] = e_sum
    e_mine = e.at[wide + z, mine]
    e_ring = along(lambda to: e_mine, e_mine, e.at[pl.ds(wide, rows - 1), mine])
    buf.t_own[...] = e_sum + carry

    carry = buf.carry[x]

    def finish(i):
        buf.back[i] = buf.local[2 * i + 1] + buf.upto[2 * i + 1] * carry

    each(0, rows, finish, 4)
    back = along(lambda to: buf.back.at[to], buf.e_own.at[z, mine], buf.e_own.at[pl.ds(0, rows - 1), mine])
    buf.e_own[z, mine] = buf.back[z]

    ring.land()
    buf.dx_send[...] = lax.fori_loop(1, rows, lambda i, s: s + buf.d_ring[i], buf.d_ring[0])
    d_across = across(buf.dx_send, buf.dx)

    e_ring.land()
    e_faces = up_down(
        (e.at[pl.ds(rows, wide), mine], e.at[rows_low, mine]), (e.at[pl.ds(wide, wide), mine], e.at[rows_high, mine]),
        e.at[rows_low, mine], e.at[rows_high, mine],
    )
    e_pair = net.move(e.at[rows_own, mine]).start(e.at[rows_own, mine], e.at[rows_own, mine], sibling)

    d_across.land()
    t_mine = buf.t_own[...]
    for group in range(groups):
        t_mine = t_mine + buf.dx[group]
    t[z, mine] = t_mine
    t_ring = along(lambda to: t.at[z, mine], t.at[z, mine], t.at[pl.ds(0, rows - 1), mine])

    def far_factors(side):
        def one(i):
            row = wide + rows + i if side == HIGH else i
            factors_x(row, buf.far[side, 0, i])
            factors_yz(row, buf.far[side, 1, i], buf.far[side, 2, i])

        each(0, wide, one, wide)

    for side, exists in ((LOW, has_low), (HIGH, has_high)):
        far_pair[side].land()
        when(exists, lambda: far_factors(side))

    e_pairs = [e_pair]
    for side, exists, where in ((LOW, has_low, rows_low), (HIGH, has_high, rows_high)):
        e_faces[side].land()
        part = e.at[where, mine]
        e_pairs.append(net.move(part, exists, exists).start(part, part, sibling))

    for pair in e_pairs:
        pair.land()

    for s in range(steps - 1):
        if s == min(3, steps - 2):
            t_ring.land()
            t_pair = net.move(t.at[:, mine]).start(t.at[:, mine], t.at[:, mine], sibling)
        if s == min(5, steps - 2):
            back.land()
            back_pair = net.move(buf.e_own.at[:, mine]).start(buf.e_own.at[:, mine], buf.e_own.at[:, mine], sibling)
        src = (e, buf.e1, buf.e2)[0 if s == 0 else 1 + (s - 1) % 2]
        dst = (buf.e1, buf.e2)[s % 2]
        reach = steps - 2 - s

        def halo_row(row, exists):
            dst[row + wide] = jnp.where(exists, stepped(src, row + wide, row), 0.0)

        def own_row(row):
            value = stepped(src, row + wide, row)
            dst[row + wide] = value
            buf.sum[row] = value if s == 0 else buf.sum[row] + value

        each(-reach, 0, lambda row: halo_row(row, has_low), rows)
        each(0, rows, own_row, rows)
        each(rows, rows + reach, lambda row: halo_row(row, has_high), rows)

    t_pair.land()
    buf.sum[...] = BETA * buf.control[...] + (t[...] + buf.sum[...]) * (1.0 / (slabs * steps))
    results = [pltpu.make_async_copy(buf.sum, gradient_out, inputs.at[0])]
    results[0].start()
    back_pair.land()

    def corrected_row(i):
        later = buf.e_own[i]
        buf.corrected[i] = guess[i] + jnp.where(core == 1, later, jnp.exp(-rate[i]) * later + buf.res[i])

    each(0, rows, corrected_row, rows)
    results.append(pltpu.make_async_copy(buf.corrected, corrected_out, inputs.at[1]))
    results[1].start()
    net.close()
    for result in results:
        result.wait()


def exchange(mesh, misfit, guess, rate, coeffs, control, rounds):
    steps, rows, mid, lanes = misfit.shape
    members, half, wide = 2 * rows, mid // 2, steps - 1
    ny = mesh.shape[SPACE]
    groups = mesh.shape[TIME] // members
    deepest = max(rounds)
    forcing_at, count = {}, 0
    for r, n in enumerate(rounds):
        for s in range(n - 1):
            forcing_at[(r, s)] = count
            count += n - 1 - s
    plane, part = (mid, lanes), (half, lanes)
    field, long, slots = (rows,) + plane, (rows + 2 * wide,) + plane, (members,) + part
    shapes = dict(
        guess=field, rate=field, control=field, corrected=field, coeffs=(3,) + field,
        cx=(2, deepest) + plane, cyz=(2, 2, max(deepest - 1, 1)) + plane,
        f_send=(2, max(count, 1)) + plane, f_halo=(2, max(count, 1)) + plane,
        rates=slots, decay=slots, upto=slots, fx_send=(2,) + part, fx=(groups, 2) + part,
        res=field, d=field, d_pair=(rows,) + part, d_chip=(rows,) + part, d_ring=(rows,) + part,
        dx_send=part, dx=(groups,) + part, t_own=part,
        terms=slots, local=slots, rx_send=(2,) + part, rx=(groups, 2) + part,
        carry=(groups,) + part, back=(rows,) + part, e_own=field, t=field, sum=field, far=(2, 3, wide) + plane,
        ax=long, bx=long, ay=long, by=long, az=long, bz=long, e=long, e1=long, e2=long,
    )
    extra = [(rows + 2 * n,) + plane for n in rounds] + [(rows + 2 * (deepest - 1),) + plane] * (deepest - 1)
    cfg = SimpleNamespace(
        names=list(shapes), steps=steps, rounds=rounds, rows=rows, mid=mid, lanes=lanes, groups=groups, ny=ny,
        forcing_at=forcing_at,
    )
    in_hbm = pl.BlockSpec(memory_space=pltpu.HBM)
    return pl.pallas_call(
        functools.partial(kernel, cfg),
        out_shape=[jax.ShapeDtypeStruct(field, F32)] * 2,
        in_specs=[in_hbm] * 5,
        out_specs=[in_hbm] * 2,
        scratch_shapes=[pltpu.VMEM(shape, F32) for shape in list(shapes.values()) + extra]
        + [pltpu.VMEM(misfit.shape, misfit.dtype), pltpu.SemaphoreType.DMA((5,))]
        + [pltpu.SemaphoreType.DMA((MAX_MOVES,))] * 2,
        compiler_params=pltpu.CompilerParams(
            collective_id=0, has_side_effects=True, vmem_limit_bytes=60 * 1024 * 1024),
        name="cycle",
    )(misfit, guess, rate, coeffs, control)


def on_device(mesh, rounds, misfit, guess, rate, coeffs, control):
    corrected, gradient = exchange(mesh, misfit, guess[0], rate[0], coeffs, control, rounds)
    return corrected[None], gradient


def solution(mesh, rounds=ROUNDS):
    slab, block = P(TIME, SPACE, None, None), P(SPACE, None, None)
    return jax.shard_map(
        functools.partial(on_device, mesh, rounds),
        mesh=mesh,
        in_specs=(slab, slab, slab, P(None, SPACE, None, None), block),
        out_specs=(slab, block),
        check_vma=False,
    )
```

```python
import functools
from types import SimpleNamespace

import jax
import jax.numpy as jnp
from jax import lax
from jax.experimental import pallas as pl
from jax.experimental.pallas import tpu as pltpu
from jax.sharding import PartitionSpec as P

NU = 0.14
BETA = 0.5
CENTRE = 1.0 - 6.0 * NU
ROUNDS = (1, 2, 2, 3)
MESH = pl.DeviceIdType.MESH
F32 = jnp.float32
MAX_MOVES = 64
LOW, HIGH = 0, 1
TIME, SPACE = "tm", "space"


def rolled(value, by, axis):
    return pltpu.roll(value, by % value.shape[axis], axis)


def when(condition, run):
    def body():
        run()

    if condition is None:
        body()
    else:
        pl.when(condition)(body)


def far_first(i, count):
    return count // 2 + jnp.where(i % 2 == 0, i // 2, -(i // 2))


class Net:
    def __init__(self, send, recv, here):
        self.send, self.recv, self.here, self.moves = send, recv, here, []

    def move(self, whole, sent=None, got=None):
        return Move(self, whole, sent, got)

    def close(self):
        for move in self.moves:
            move.close()


class Move:
    def __init__(self, net, whole, sent, got):
        self.net, self.whole, self.sent, self.got = net, whole, sent, got
        self.index, self.started, self.arrived = len(net.moves), False, False
        net.moves.append(self)

    def copy(self, src, dst, device):
        return pltpu.make_async_remote_copy(
            src_ref=src, dst_ref=dst, send_sem=self.net.send.at[self.index], recv_sem=self.net.recv.at[self.index],
            device_id=device, device_id_type=MESH,
        )

    def start(self, src, dst, device):
        self.started = True
        when(self.sent, lambda: self.copy(src, dst, device).start())
        return self

    def land(self):
        self.arrived = True
        when(self.got, lambda: self.copy(self.whole, self.whole, self.net.here).wait_recv())

    def close(self):
        if self.started:
            if not self.arrived:
                self.land()
            when(self.sent, lambda: self.copy(self.whole, self.whole, self.net.here).wait_send())


def kernel(cfg, misfit_in, guess_in, rate_in, coeffs_in, control_in, corrected_out, gradient_out, *scratch):
    buf = SimpleNamespace(**dict(zip(cfg.names, scratch)))
    wf = scratch[len(cfg.names):len(cfg.names) + len(cfg.rounds)]
    mids = scratch[len(cfg.names) + len(cfg.rounds):-4]
    misfit, inputs = scratch[-4], scratch[-3]
    guess, rate, coeffs = buf.guess, buf.rate, buf.coeffs
    fetches = [
        pltpu.make_async_copy(src, dst, inputs.at[i])
        for i, (src, dst) in enumerate(((guess_in, guess), (coeffs_in, coeffs), (misfit_in, misfit), (rate_in, rate), (control_in, buf.control)))
    ]
    for fetch in fetches:
        fetch.start()
    steps, rounds, rows, mid, lanes = cfg.steps, cfg.rounds, cfg.rows, cfg.mid, cfg.lanes
    groups, ny = cfg.groups, cfg.ny
    half, members, wide = mid // 2, 2 * rows, steps - 1
    deepest = max(rounds)
    slabs = groups * members

    tm, y = lax.axis_index(TIME), lax.axis_index(SPACE)
    x, spot = tm // members, tm % members
    z, core = spot // 2, spot % 2
    base = x * members
    has_low, has_high = y > 0, y < ny - 1
    has_next, has_before = tm < slabs - 1, tm > 0
    below, above, sibling = (tm, y - 1), (tm, y + 1), (base + spot + 1 - 2 * core, y)

    net = Net(scratch[-2], scratch[-1], (tm, y))
    ax, bx, ay, by, az, bz = buf.ax, buf.bx, buf.ay, buf.by, buf.az, buf.bz
    mine = pl.ds(pl.multiple_of(core * half, half), half)
    other = pl.ds(pl.multiple_of((1 - core) * half, half), half)
    rows_own, rows_low, rows_high = pl.ds(wide, rows), pl.ds(0, wide), pl.ds(wide + rows, wide)

    barrier = pltpu.get_barrier_semaphore()

    def greet(device):
        pl.semaphore_signal(barrier, inc=1, device_id=device, device_id_type=MESH)

    def greet_member(i, _):
        greet((base + (spot + i) % members, y))
        return 0

    when(has_low, lambda: greet(below))
    when(has_high, lambda: greet(above))
    for exists, there in ((has_next, tm + 1), (has_before, tm - 1)):
        when(exists, lambda: greet((there, y)))
        when(exists & has_low, lambda: greet((there, y - 1)))
        when(exists & has_high, lambda: greet((there, y + 1)))
    lax.fori_loop(1, members, greet_member, 0)
    for i in range(1, groups):
        greet(((x + i) % groups * members + spot, y))
    sides = has_low.astype(jnp.int32) + has_high.astype(jnp.int32)
    ends = has_next.astype(jnp.int32) + has_before.astype(jnp.int32)

    for fetch in fetches:
        fetch.wait()
    for r, n in enumerate(rounds):
        for s in range(n - 1):
            k, turn, width = cfg.forcing_at[(r, s)], sum(rounds[:r]) + s, n - 1 - s
            for i in range(width):
                buf.f_send[LOW, k + i] = misfit[steps - 1 - turn, rows - width + i].astype(F32)
                buf.f_send[HIGH, k + i] = misfit[steps - 1 - turn, i].astype(F32)

    pl.semaphore_wait(barrier, members - 1 + groups - 1 + sides + ends + sides * ends)

    first = rounds[0]
    start = net.move(wf[0].at[pl.ds(first, rows)], has_before, has_next)
    start.start(guess, wf[0].at[pl.ds(first, rows)], (tm - 1, y))

    def up_down(low, high, whole_low, whole_high):
        up = net.move(whole_low, has_high, has_low)
        down = net.move(whole_high, has_low, has_high)
        up.start(low[0], low[1], above)
        down.start(high[0], high[1], below)
        return up, down

    lows, highs = wf[0].at[pl.ds(0, first)], wf[0].at[pl.ds(first + rows, first)]
    start_up = net.move(lows, has_before & has_high, has_next & has_low)
    start_up.start(guess.at[pl.ds(rows - first, first)], lows, (tm - 1, y + 1))
    start_down = net.move(highs, has_before & has_low, has_next & has_high)
    start_down.start(guess.at[pl.ds(0, first)], highs, (tm - 1, y - 1))
    start_faces = (start_up, start_down)

    def both_ends(src, at_low, at_high, dst):
        return up_down((src.at[at_high], dst.at[LOW]), (src.at[at_low], dst.at[HIGH]), dst.at[LOW], dst.at[HIGH])

    def ends(src, at, width, low_halo, high_halo, depth):
        up, down = low_halo.at[pl.ds(depth - at - width, width)], high_halo.at[pl.ds(at, width)]
        return up_down((src.at[pl.ds(rows - at - width, width)], up), (src.at[pl.ds(at, width)], down), up, down)

    def reach_of(r):
        before = max((0,) + rounds[:r])
        after = max(before, rounds[r])
        return before, after, max(before - 1, 0), after - 1

    def near_stage(r):
        before, after, yz_before, yz_after = reach_of(r)
        moves = []
        if after > before:
            moves.append(ends(coeffs.at[0], before, after - before, buf.cx.at[LOW], buf.cx.at[HIGH], deepest))
        if yz_after > yz_before:
            for i in range(2):
                moves.append(ends(coeffs.at[1 + i], yz_before, yz_after - yz_before, buf.cyz.at[LOW, i], buf.cyz.at[HIGH, i],
                                  deepest - 1))
        n = rounds[r]
        if n > 1:
            part = pl.ds(cfg.forcing_at[(r, 0)], n * (n - 1) // 2)
            low, high = buf.f_halo.at[LOW, part], buf.f_halo.at[HIGH, part]
            moves.append(up_down((buf.f_send.at[LOW, part], low), (buf.f_send.at[HIGH, part], high), low, high))
        return moves

    near = [near_stage(r) for r in range(min(2, len(rounds)))]

    def transpose(src, dst):
        move = net.move(dst.at[pl.ds(0, members - 1)])

        def send(i, _):
            to = (spot + far_first(i, members)) % members
            part = src.at[to // 2, pl.ds(pl.multiple_of(to % 2 * half, half), half)]
            move.start(part, dst.at[spot], (base + to, y))
            return 0

        lax.fori_loop(1, members, send, 0)
        dst[spot] = src[z, mine]
        return move

    def across(src, dst):
        move = net.move(dst.at[pl.ds(0, groups - 1)])
        for i in range(1, groups):
            move.start(src, dst.at[x], ((x + i) % groups * members + spot, y))
        dst[x] = src[...]
        return move

    def along(source, target, whole):
        move = net.move(whole)

        def send(i, _):
            to = (z + far_first(i, rows)) % rows
            move.start(source(to), target, (base + 2 * to + core, y))
            return 0

        lax.fori_loop(1, rows, send, 0)
        return move

    def factors_x(row, c):
        ax[row] = NU + 0.5 * c
        bx[row] = NU - 0.5 * c

    def factors_yz(row, cy, cz):
        place = lax.broadcasted_iota(jnp.int32, (mid, lanes), 0)
        ay[row] = jnp.where(place == 0, 0.0, NU + 0.5 * cy)
        by[row] = jnp.where(place == mid - 1, 0.0, NU - 0.5 * cy)
        place = lax.broadcasted_iota(jnp.int32, (mid, lanes), 1)
        az[row] = jnp.where(place == 0, 0.0, NU + 0.5 * cz)
        bz[row] = jnp.where(place == lanes - 1, 0.0, NU - 0.5 * cz)

    def each(start, stop, run, unroll=1):
        def one(i, _):
            run(i)
            return 0

        if stop > start:
            lax.fori_loop(start, stop, one, 0, unroll=min(unroll, stop - start))

    def own_factors(i):
        factors_x(wide + i, coeffs[0, i])
        factors_yz(wide + i, coeffs[1, i], coeffs[2, i])

    each(0, rows, own_factors, 4)

    def clear(ref, start, count):
        def one(i):
            ref[i] = jnp.zeros((mid, lanes), F32)

        each(start, start + count, one)

    halos = [(ref, n) for ref, n in zip(wf[1:], rounds[1:])] + [(buf.e, wide), (buf.e1, wide), (buf.e2, wide)]

    @pl.when(jnp.logical_not(has_low))
    def _():
        clear(bx, 0, wide)
        for ref, n in halos:
            clear(ref, 0, n)

    @pl.when(jnp.logical_not(has_high))
    def _():
        clear(ax, wide + rows, wide)
        for ref, n in halos:
            clear(ref, n + rows, n)

    when(jnp.logical_not(has_next & has_low), lambda: clear(wf[0], 0, first))
    when(jnp.logical_not(has_next & has_high), lambda: clear(wf[0], first + rows, first))
    when(jnp.logical_not(has_next), lambda: clear(wf[0], first, rows))

    def stepped(src, at, row):
        w = src[at]
        place = row + wide
        value = CENTRE * w
        value = value + (ax[place + 1] * src[at + 1] + bx[place - 1] * src[at - 1])
        value = value + (rolled(ay[place] * w, -1, 0) + rolled(by[place] * w, 1, 0))
        return value + (rolled(az[place] * w, -1, 1) + rolled(bz[place] * w, 1, 1))

    def relax_row(r, s, row, side=None):
        n = rounds[r]
        turn = sum(rounds[:r]) + s
        src, shift = (wf[r], n) if s == 0 else (mids[s - 1], deepest - 1)
        if side is None:
            forcing = misfit[steps - 1 - turn, row].astype(F32)
        elif side == LOW:
            forcing = buf.f_halo[LOW, cfg.forcing_at[(r, s)] + (n - 1 - s) + row]
        else:
            forcing = buf.f_halo[HIGH, cfg.forcing_at[(r, s)] + row - rows]
        value = stepped(src, row + shift, row) + forcing
        if side is not None:
            value = jnp.where(has_low if side == LOW else has_high, value, 0.0)
        if s < n - 1:
            mids[s][row + deepest - 1] = value
        elif r < len(rounds) - 1:
            wf[r + 1][row + rounds[r + 1]] = value
        if side is None:
            if turn == 0:
                buf.d[row] = guess[row] + value
            elif turn < steps - 1:
                buf.d[row] = buf.d[row] + value
            else:
                buf.res[row] = value - guess[row]

    def inner(r):
        for s in range(rounds[r]):
            each(s + 1, rows - 1 - s, lambda row: relax_row(r, s, row), rows)

    def outer(r):
        for s in range(rounds[r]):
            reach = rounds[r] - 1 - s
            for i in range(reach):
                relax_row(r, s, -1 - i, LOW)
                relax_row(r, s, rows + i, HIGH)
            for i in range(s + 1):
                relax_row(r, s, i)
                relax_row(r, s, rows - 1 - i)

    def near_factors(r, side):
        before, after, yz_before, yz_after = reach_of(r)
        for k in range(before, after):
            if side == HIGH:
                factors_x(wide + rows + k, buf.cx[HIGH, k])
            else:
                factors_x(wide - 1 - k, buf.cx[LOW, deepest - 1 - k])
        for k in range(yz_before, yz_after):
            if side == HIGH:
                factors_yz(wide + rows + k, buf.cyz[HIGH, 0, k], buf.cyz[HIGH, 1, k])
            else:
                factors_yz(wide - 1 - k, buf.cyz[LOW, 0, deepest - 2 - k], buf.cyz[LOW, 1, deepest - 2 - k])

    def decays():
        rates.land()
        last = members - 1
        factor = jnp.exp(-buf.rates[last])
        buf.decay[last] = factor
        buf.upto[last] = factor

        def one(i, carry):
            upto, summed = carry
            k = last - i
            factor = jnp.exp(-buf.rates[k])
            upto = factor * upto
            buf.decay[k] = factor
            buf.upto[k] = upto
            return upto, summed + jnp.where((k > 0) | (x > 0), upto, 0.0)

        buf.fx_send[0], buf.fx_send[1] = lax.fori_loop(1, members, one, (factor, factor), unroll=3)
        return across(buf.fx_send, buf.fx)

    start.land()
    faces = start_faces
    for r in range(len(rounds)):
        inner(r)
        if r < len(rounds) - 1:
            n, ref = rounds[r + 1], wf[r + 1]
            low, high = ref.at[pl.ds(0, n)], ref.at[pl.ds(n + rows, n)]
            coming = net.move(low, has_high, has_low), net.move(high, has_low, has_high)
        for side, exists in ((LOW, has_low), (HIGH, has_high)):
            for pair in near[r]:
                pair[side].land()
            if near[r]:
                when(exists, lambda: near_factors(r, side))
            faces[side].land()
        outer(r)
        if r < len(rounds) - 1:
            coming[HIGH].start(ref.at[pl.ds(n, n)], high, below)
            coming[LOW].start(ref.at[pl.ds(rows, n)], low, above)
            if r + 2 < len(rounds):
                near.append(near_stage(r + 2))
        if r == 0:
            rates = transpose(rate, buf.rates)
        if r < len(rounds) - 1:
            faces = coming

    terms = transpose(buf.res, buf.terms)
    pair = net.move(buf.d_pair).start(buf.d.at[:, other], buf.d_pair, sibling)
    far = up_down(
        (coeffs.at[:, pl.ds(rows - wide, wide), mine], buf.far.at[LOW, :, :, mine]),
        (coeffs.at[:, pl.ds(0, wide), mine], buf.far.at[HIGH, :, :, mine]),
        buf.far.at[LOW, :, :, mine], buf.far.at[HIGH, :, :, mine],
    )

    group_decay = decays()

    terms.land()
    last = members - 1
    value = buf.terms[last]
    buf.local[last] = value

    def solve(i, carry):
        value, summed = carry
        k = last - i
        value = buf.decay[k] * value + buf.terms[k]
        buf.local[k] = value
        return value, summed + jnp.where((k > 0) | (x > 0), value, 0.0)

    buf.rx_send[0], buf.rx_send[1] = lax.fori_loop(1, members, solve, (value, value), unroll=5)
    group_result = across(buf.rx_send, buf.rx)

    pair.land()

    def pair_sum(i):
        buf.d_chip[i] = buf.d[i, mine] + buf.d_pair[i]

    each(0, rows, pair_sum, rows)
    ring = along(lambda to: buf.d_chip.at[to], buf.d_ring.at[z], buf.d_ring.at[pl.ds(0, rows - 1)])
    buf.d_ring[z] = buf.d_chip[z]

    far_pair = []
    for side, exists in ((LOW, has_low), (HIGH, has_high)):
        far[side].land()
        part = buf.far.at[side, :, :, mine]
        far_pair.append(net.move(part, exists, exists).start(part, part, sibling))

    group_decay.land()
    group_result.land()
    carry = jnp.zeros((half, lanes), F32)
    e_sum = carry
    for group in reversed(range(groups)):
        buf.carry[group] = carry
        e_sum = e_sum + (buf.rx[group, 1] + buf.fx[group, 1] * carry)
        carry = buf.rx[group, 0] + buf.fx[group, 0] * carry
    e, t = buf.e, buf.t
    e[wide + z, mine] = e_sum
    e_mine = e.at[wide + z, mine]
    e_ring = along(lambda to: e_mine, e_mine, e.at[pl.ds(wide, rows - 1), mine])
    buf.t_own[...] = e_sum + carry

    carry = buf.carry[x]

    def finish(i):
        buf.back[i] = buf.local[2 * i + 1] + buf.upto[2 * i + 1] * carry

    each(0, rows, finish, 4)
    back = along(lambda to: buf.back.at[to], buf.e_own.at[z, mine], buf.e_own.at[pl.ds(0, rows - 1), mine])
    buf.e_own[z, mine] = buf.back[z]

    ring.land()
    buf.dx_send[...] = lax.fori_loop(1, rows, lambda i, s: s + buf.d_ring[i], buf.d_ring[0])
    d_across = across(buf.dx_send, buf.dx)

    e_ring.land()
    e_faces = up_down(
        (e.at[pl.ds(rows, wide), mine], e.at[rows_low, mine]), (e.at[pl.ds(wide, wide), mine], e.at[rows_high, mine]),
        e.at[rows_low, mine], e.at[rows_high, mine],
    )
    e_pair = net.move(e.at[rows_own, mine]).start(e.at[rows_own, mine], e.at[rows_own, mine], sibling)

    d_across.land()
    t_mine = buf.t_own[...]
    for group in range(groups):
        t_mine = t_mine + buf.dx[group]
    t[z, mine] = t_mine
    t_ring = along(lambda to: t.at[z, mine], t.at[z, mine], t.at[pl.ds(0, rows - 1), mine])

    def far_factors(side):
        def one(i):
            row = wide + rows + i if side == HIGH else i
            factors_x(row, buf.far[side, 0, i])
            factors_yz(row, buf.far[side, 1, i], buf.far[side, 2, i])

        each(0, wide, one, wide)

    for side, exists in ((LOW, has_low), (HIGH, has_high)):
        far_pair[side].land()
        when(exists, lambda: far_factors(side))

    e_pairs = [e_pair]
    for side, exists, where in ((LOW, has_low, rows_low), (HIGH, has_high, rows_high)):
        e_faces[side].land()
        part = e.at[where, mine]
        e_pairs.append(net.move(part, exists, exists).start(part, part, sibling))

    for pair in e_pairs:
        pair.land()

    for s in range(steps - 1):
        if s == min(3, steps - 2):
            t_ring.land()
            t_pair = net.move(t.at[:, mine]).start(t.at[:, mine], t.at[:, mine], sibling)
        if s == min(5, steps - 2):
            back.land()
            back_pair = net.move(buf.e_own.at[:, mine]).start(buf.e_own.at[:, mine], buf.e_own.at[:, mine], sibling)
        src = (e, buf.e1, buf.e2)[0 if s == 0 else 1 + (s - 1) % 2]
        dst = (buf.e1, buf.e2)[s % 2]
        reach = steps - 2 - s

        def halo_row(row, exists):
            dst[row + wide] = jnp.where(exists, stepped(src, row + wide, row), 0.0)

        def own_row(row):
            value = stepped(src, row + wide, row)
            dst[row + wide] = value
            buf.sum[row] = value if s == 0 else buf.sum[row] + value

        each(-reach, 0, lambda row: halo_row(row, has_low), rows)
        each(0, rows, own_row, rows)
        each(rows, rows + reach, lambda row: halo_row(row, has_high), rows)

    t_pair.land()
    buf.sum[...] = BETA * buf.control[...] + (t[...] + buf.sum[...]) * (1.0 / (slabs * steps))
    results = [pltpu.make_async_copy(buf.sum, gradient_out, inputs.at[0])]
    results[0].start()
    back_pair.land()

    def corrected_row(i):
        later = buf.e_own[i]
        buf.corrected[i] = guess[i] + jnp.where(core == 1, later, jnp.exp(-rate[i]) * later + buf.res[i])

    each(0, rows, corrected_row, rows)
    results.append(pltpu.make_async_copy(buf.corrected, corrected_out, inputs.at[1]))
    results[1].start()
    net.close()
    for result in results:
        result.wait()


def exchange(mesh, misfit, guess, rate, coeffs, control, rounds):
    steps, rows, mid, lanes = misfit.shape
    members, half, wide = 2 * rows, mid // 2, steps - 1
    ny = mesh.shape[SPACE]
    groups = mesh.shape[TIME] // members
    deepest = max(rounds)
    forcing_at, count = {}, 0
    for r, n in enumerate(rounds):
        for s in range(n - 1):
            forcing_at[(r, s)] = count
            count += n - 1 - s
    plane, part = (mid, lanes), (half, lanes)
    field, long, slots = (rows,) + plane, (rows + 2 * wide,) + plane, (members,) + part
    shapes = dict(
        guess=field, rate=field, control=field, corrected=field, coeffs=(3,) + field,
        cx=(2, deepest) + plane, cyz=(2, 2, max(deepest - 1, 1)) + plane,
        f_send=(2, max(count, 1)) + plane, f_halo=(2, max(count, 1)) + plane,
        rates=slots, decay=slots, upto=slots, fx_send=(2,) + part, fx=(groups, 2) + part,
        res=field, d=field, d_pair=(rows,) + part, d_chip=(rows,) + part, d_ring=(rows,) + part,
        dx_send=part, dx=(groups,) + part, t_own=part,
        terms=slots, local=slots, rx_send=(2,) + part, rx=(groups, 2) + part,
        carry=(groups,) + part, back=(rows,) + part, e_own=field, t=field, sum=field, far=(2, 3, wide) + plane,
        ax=long, bx=long, ay=long, by=long, az=long, bz=long, e=long, e1=long, e2=long,
    )
    extra = [(rows + 2 * n,) + plane for n in rounds] + [(rows + 2 * (deepest - 1),) + plane] * (deepest - 1)
    cfg = SimpleNamespace(
        names=list(shapes), steps=steps, rounds=rounds, rows=rows, mid=mid, lanes=lanes, groups=groups, ny=ny,
        forcing_at=forcing_at,
    )
    in_hbm = pl.BlockSpec(memory_space=pltpu.HBM)
    return pl.pallas_call(
        functools.partial(kernel, cfg),
        out_shape=[jax.ShapeDtypeStruct(field, F32)] * 2,
        in_specs=[in_hbm] * 5,
        out_specs=[in_hbm] * 2,
        scratch_shapes=[pltpu.VMEM(shape, F32) for shape in list(shapes.values()) + extra]
        + [pltpu.VMEM(misfit.shape, misfit.dtype), pltpu.SemaphoreType.DMA((5,))]
        + [pltpu.SemaphoreType.DMA((MAX_MOVES,))] * 2,
        compiler_params=pltpu.CompilerParams(
            collective_id=0, has_side_effects=True, vmem_limit_bytes=213 * 256 * 1024),
        name="cycle",
    )(misfit, guess, rate, coeffs, control)


def on_device(mesh, rounds, misfit, guess, rate, coeffs, control):
    corrected, gradient = exchange(mesh, misfit, guess[0], rate[0], coeffs, control, rounds)
    return corrected[None], gradient


def solution(mesh, rounds=ROUNDS):
    slab, block = P(TIME, SPACE, None, None), P(SPACE, None, None)
    return jax.shard_map(
        functools.partial(on_device, mesh, rounds),
        mesh=mesh,
        in_specs=(slab, slab, slab, P(None, SPACE, None, None), block),
        out_specs=(slab, block),
        check_vma=False,
    )
```

```python
import functools
from types import SimpleNamespace

import jax
import jax.numpy as jnp
from jax import lax
from jax.experimental import pallas as pl
from jax.experimental.pallas import tpu as pltpu
from jax.sharding import PartitionSpec as P

NU = 0.14
BETA = 0.5
CENTRE = 1.0 - 6.0 * NU
ROUNDS = (1, 2, 2, 3)
MESH = pl.DeviceIdType.MESH
F32 = jnp.float32
MAX_MOVES = 64
LOW, HIGH = 0, 1
TIME, SPACE = "tm", "space"


def rolled(value, by, axis):
    return pltpu.roll(value, by % value.shape[axis], axis)


def when(condition, run):
    def body():
        run()

    if condition is None:
        body()
    else:
        pl.when(condition)(body)


def far_first(i, count):
    return count // 2 + jnp.where(i % 2 == 0, i // 2, -(i // 2))


class Net:
    def __init__(self, send, recv, here):
        self.send, self.recv, self.here, self.moves = send, recv, here, []

    def move(self, whole, sent=None, got=None):
        return Move(self, whole, sent, got)

    def close(self):
        for move in self.moves:
            move.close()


class Move:
    def __init__(self, net, whole, sent, got):
        self.net, self.whole, self.sent, self.got = net, whole, sent, got
        self.index, self.started, self.arrived = len(net.moves), False, False
        net.moves.append(self)

    def copy(self, src, dst, device):
        return pltpu.make_async_remote_copy(
            src_ref=src, dst_ref=dst, send_sem=self.net.send.at[self.index], recv_sem=self.net.recv.at[self.index],
            device_id=device, device_id_type=MESH,
        )

    def start(self, src, dst, device):
        self.started = True
        when(self.sent, lambda: self.copy(src, dst, device).start())
        return self

    def land(self):
        self.arrived = True
        when(self.got, lambda: self.copy(self.whole, self.whole, self.net.here).wait_recv())

    def close(self):
        if self.started:
            if not self.arrived:
                self.land()
            when(self.sent, lambda: self.copy(self.whole, self.whole, self.net.here).wait_send())


def kernel(cfg, misfit_in, guess_in, rate_in, coeffs_in, control_in, corrected_out, gradient_out, *scratch):
    buf = SimpleNamespace(**dict(zip(cfg.names, scratch)))
    wf = scratch[len(cfg.names):len(cfg.names) + len(cfg.rounds)]
    mids = scratch[len(cfg.names) + len(cfg.rounds):-4]
    misfit, inputs = scratch[-4], scratch[-3]
    guess, rate, coeffs = buf.guess, buf.rate, buf.coeffs
    fetches = [
        pltpu.make_async_copy(src, dst, inputs.at[i])
        for i, (src, dst) in enumerate(((guess_in, guess), (coeffs_in, coeffs), (misfit_in, misfit), (rate_in, rate), (control_in, buf.control)))
    ]
    for fetch in fetches:
        fetch.start()
    steps, rounds, rows, mid, lanes = cfg.steps, cfg.rounds, cfg.rows, cfg.mid, cfg.lanes
    groups, ny = cfg.groups, cfg.ny
    half, members, wide = mid // 2, 2 * rows, steps - 1
    deepest = max(rounds)
    slabs = groups * members

    tm, y = lax.axis_index(TIME), lax.axis_index(SPACE)
    x, spot = tm // members, tm % members
    z, core = spot // 2, spot % 2
    base = x * members
    has_low, has_high = y > 0, y < ny - 1
    has_next, has_before = tm < slabs - 1, tm > 0
    below, above, sibling = (tm, y - 1), (tm, y + 1), (base + spot + 1 - 2 * core, y)

    net = Net(scratch[-2], scratch[-1], (tm, y))
    ax, bx, ay, by, az, bz = buf.ax, buf.bx, buf.ay, buf.by, buf.az, buf.bz
    mine = pl.ds(pl.multiple_of(core * half, half), half)
    other = pl.ds(pl.multiple_of((1 - core) * half, half), half)
    rows_own, rows_low, rows_high = pl.ds(wide, rows), pl.ds(0, wide), pl.ds(wide + rows, wide)

    barrier = pltpu.get_barrier_semaphore()

    def greet(device):
        pl.semaphore_signal(barrier, inc=1, device_id=device, device_id_type=MESH)

    def greet_member(i, _):
        greet((base + (spot + far_first(i, members)) % members, y))
        return 0

    lax.fori_loop(1, members, greet_member, 0, unroll=members - 1)
    for i in range(1, groups):
        greet(((x + i) % groups * members + spot, y))
    when(has_low, lambda: greet(below))
    when(has_high, lambda: greet(above))
    for exists, there in ((has_next, tm + 1), (has_before, tm - 1)):
        when(exists, lambda: greet((there, y)))
        when(exists & has_low, lambda: greet((there, y - 1)))
        when(exists & has_high, lambda: greet((there, y + 1)))
    sides = has_low.astype(jnp.int32) + has_high.astype(jnp.int32)
    ends = has_next.astype(jnp.int32) + has_before.astype(jnp.int32)

    for fetch in fetches:
        fetch.wait()
    for r, n in enumerate(rounds):
        for s in range(n - 1):
            k, turn, width = cfg.forcing_at[(r, s)], sum(rounds[:r]) + s, n - 1 - s
            for i in range(width):
                buf.f_send[LOW, k + i] = misfit[steps - 1 - turn, rows - width + i].astype(F32)
                buf.f_send[HIGH, k + i] = misfit[steps - 1 - turn, i].astype(F32)

    pl.semaphore_wait(barrier, members - 1 + groups - 1 + sides + ends + sides * ends)

    first = rounds[0]
    start = net.move(wf[0].at[pl.ds(first, rows)], has_before, has_next)
    start.start(guess, wf[0].at[pl.ds(first, rows)], (tm - 1, y))

    def up_down(low, high, whole_low, whole_high):
        up = net.move(whole_low, has_high, has_low)
        down = net.move(whole_high, has_low, has_high)
        up.start(low[0], low[1], above)
        down.start(high[0], high[1], below)
        return up, down

    lows, highs = wf[0].at[pl.ds(0, first)], wf[0].at[pl.ds(first + rows, first)]
    start_up = net.move(lows, has_before & has_high, has_next & has_low)
    start_up.start(guess.at[pl.ds(rows - first, first)], lows, (tm - 1, y + 1))
    start_down = net.move(highs, has_before & has_low, has_next & has_high)
    start_down.start(guess.at[pl.ds(0, first)], highs, (tm - 1, y - 1))
    start_faces = (start_up, start_down)

    def both_ends(src, at_low, at_high, dst):
        return up_down((src.at[at_high], dst.at[LOW]), (src.at[at_low], dst.at[HIGH]), dst.at[LOW], dst.at[HIGH])

    def ends(src, at, width, low_halo, high_halo, depth):
        up, down = low_halo.at[pl.ds(depth - at - width, width)], high_halo.at[pl.ds(at, width)]
        return up_down((src.at[pl.ds(rows - at - width, width)], up), (src.at[pl.ds(at, width)], down), up, down)

    def reach_of(r):
        before = max((0,) + rounds[:r])
        after = max(before, rounds[r])
        return before, after, max(before - 1, 0), after - 1

    def near_stage(r):
        before, after, yz_before, yz_after = reach_of(r)
        moves = []
        if after > before:
            moves.append(ends(coeffs.at[0], before, after - before, buf.cx.at[LOW], buf.cx.at[HIGH], deepest))
        if yz_after > yz_before:
            for i in range(2):
                moves.append(ends(coeffs.at[1 + i], yz_before, yz_after - yz_before, buf.cyz.at[LOW, i], buf.cyz.at[HIGH, i],
                                  deepest - 1))
        n = rounds[r]
        if n > 1:
            part = pl.ds(cfg.forcing_at[(r, 0)], n * (n - 1) // 2)
            low, high = buf.f_halo.at[LOW, part], buf.f_halo.at[HIGH, part]
            moves.append(up_down((buf.f_send.at[LOW, part], low), (buf.f_send.at[HIGH, part], high), low, high))
        return moves

    near = [near_stage(r) for r in range(min(2, len(rounds)))]

    def transpose(src, dst):
        move = net.move(dst.at[pl.ds(0, members - 1)])

        def send(i, _):
            to = (spot + far_first(i, members)) % members
            part = src.at[to // 2, pl.ds(pl.multiple_of(to % 2 * half, half), half)]
            move.start(part, dst.at[spot], (base + to, y))
            return 0

        lax.fori_loop(1, members, send, 0)
        dst[spot] = src[z, mine]
        return move

    def across(src, dst):
        move = net.move(dst.at[pl.ds(0, groups - 1)])
        for i in sorted(range(1, groups), key=lambda i: -min(i, groups - i)):
            move.start(src, dst.at[x], ((x + i) % groups * members + spot, y))
        dst[x] = src[...]
        return move

    def along(source, target, whole):
        move = net.move(whole)

        def send(i, _):
            to = (z + far_first(i, rows)) % rows
            move.start(source(to), target, (base + 2 * to + core, y))
            return 0

        lax.fori_loop(1, rows, send, 0)
        return move

    def factors_x(row, c):
        ax[row] = NU + 0.5 * c
        bx[row] = NU - 0.5 * c

    def factors_yz(row, cy, cz):
        place = lax.broadcasted_iota(jnp.int32, (mid, lanes), 0)
        ay[row] = jnp.where(place == 0, 0.0, NU + 0.5 * cy)
        by[row] = jnp.where(place == mid - 1, 0.0, NU - 0.5 * cy)
        place = lax.broadcasted_iota(jnp.int32, (mid, lanes), 1)
        az[row] = jnp.where(place == 0, 0.0, NU + 0.5 * cz)
        bz[row] = jnp.where(place == lanes - 1, 0.0, NU - 0.5 * cz)

    def each(start, stop, run, unroll=1):
        def one(i, _):
            run(i)
            return 0

        if stop > start:
            lax.fori_loop(start, stop, one, 0, unroll=min(unroll, stop - start))

    def own_factors(i):
        factors_x(wide + i, coeffs[0, i])
        factors_yz(wide + i, coeffs[1, i], coeffs[2, i])

    each(0, rows, own_factors, 4)

    def clear(ref, start, count):
        def one(i):
            ref[i] = jnp.zeros((mid, lanes), F32)

        each(start, start + count, one)

    halos = [(ref, n) for ref, n in zip(wf[1:], rounds[1:])] + [(buf.e, wide), (buf.e1, wide), (buf.e2, wide)]

    @pl.when(jnp.logical_not(has_low))
    def _():
        clear(bx, 0, wide)
        for ref, n in halos:
            clear(ref, 0, n)

    @pl.when(jnp.logical_not(has_high))
    def _():
        clear(ax, wide + rows, wide)
        for ref, n in halos:
            clear(ref, n + rows, n)

    when(jnp.logical_not(has_next & has_low), lambda: clear(wf[0], 0, first))
    when(jnp.logical_not(has_next & has_high), lambda: clear(wf[0], first + rows, first))
    when(jnp.logical_not(has_next), lambda: clear(wf[0], first, rows))

    def stepped(src, at, row):
        w = src[at]
        place = row + wide
        value = CENTRE * w
        value = value + (ax[place + 1] * src[at + 1] + bx[place - 1] * src[at - 1])
        value = value + (rolled(ay[place] * w, -1, 0) + rolled(by[place] * w, 1, 0))
        return value + (rolled(az[place] * w, -1, 1) + rolled(bz[place] * w, 1, 1))

    def relax_row(r, s, row, side=None):
        n = rounds[r]
        turn = sum(rounds[:r]) + s
        src, shift = (wf[r], n) if s == 0 else (mids[s - 1], deepest - 1)
        if side is None:
            forcing = misfit[steps - 1 - turn, row].astype(F32)
        elif side == LOW:
            forcing = buf.f_halo[LOW, cfg.forcing_at[(r, s)] + (n - 1 - s) + row]
        else:
            forcing = buf.f_halo[HIGH, cfg.forcing_at[(r, s)] + row - rows]
        value = stepped(src, row + shift, row) + forcing
        if side is not None:
            value = jnp.where(has_low if side == LOW else has_high, value, 0.0)
        if s < n - 1:
            mids[s][row + deepest - 1] = value
        elif r < len(rounds) - 1:
            wf[r + 1][row + rounds[r + 1]] = value
        if side is None:
            if turn == 0:
                buf.d[row] = guess[row] + value
            elif turn < steps - 1:
                buf.d[row] = buf.d[row] + value
            else:
                buf.res[row] = value - guess[row]

    def inner(r):
        for s in range(rounds[r]):
            each(s + 1, rows - 1 - s, lambda row: relax_row(r, s, row), rows)

    def outer(r):
        for s in range(rounds[r]):
            reach = rounds[r] - 1 - s
            for i in range(reach):
                relax_row(r, s, -1 - i, LOW)
                relax_row(r, s, rows + i, HIGH)
            for i in range(s + 1):
                relax_row(r, s, i)
                relax_row(r, s, rows - 1 - i)

    def near_factors(r, side):
        before, after, yz_before, yz_after = reach_of(r)
        for k in range(before, after):
            if side == HIGH:
                factors_x(wide + rows + k, buf.cx[HIGH, k])
            else:
                factors_x(wide - 1 - k, buf.cx[LOW, deepest - 1 - k])
        for k in range(yz_before, yz_after):
            if side == HIGH:
                factors_yz(wide + rows + k, buf.cyz[HIGH, 0, k], buf.cyz[HIGH, 1, k])
            else:
                factors_yz(wide - 1 - k, buf.cyz[LOW, 0, deepest - 2 - k], buf.cyz[LOW, 1, deepest - 2 - k])

    def decays():
        rates.land()
        last = members - 1
        factor = jnp.exp(-buf.rates[last])
        buf.decay[last] = factor
        buf.upto[last] = factor

        def one(i, carry):
            upto, summed = carry
            k = last - i
            factor = jnp.exp(-buf.rates[k])
            upto = factor * upto
            buf.decay[k] = factor
            buf.upto[k] = upto
            return upto, summed + jnp.where((k > 0) | (x > 0), upto, 0.0)

        buf.fx_send[0], buf.fx_send[1] = lax.fori_loop(1, members, one, (factor, factor), unroll=3)
        return across(buf.fx_send, buf.fx)

    start.land()
    faces = start_faces
    for r in range(len(rounds)):
        inner(r)
        if r < len(rounds) - 1:
            n, ref = rounds[r + 1], wf[r + 1]
            low, high = ref.at[pl.ds(0, n)], ref.at[pl.ds(n + rows, n)]
            coming = net.move(low, has_high, has_low), net.move(high, has_low, has_high)
        for side, exists in ((LOW, has_low), (HIGH, has_high)):
            for pair in near[r]:
                pair[side].land()
            if near[r]:
                when(exists, lambda: near_factors(r, side))
            faces[side].land()
        outer(r)
        if r < len(rounds) - 1:
            coming[HIGH].start(ref.at[pl.ds(n, n)], high, below)
            coming[LOW].start(ref.at[pl.ds(rows, n)], low, above)
            if r + 2 < len(rounds):
                near.append(near_stage(r + 2))
        if r == 0:
            rates = transpose(rate, buf.rates)
        if r < len(rounds) - 1:
            faces = coming

    terms = transpose(buf.res, buf.terms)
    pair = net.move(buf.d_pair).start(buf.d.at[:, other], buf.d_pair, sibling)
    far = up_down(
        (coeffs.at[:, pl.ds(rows - wide, wide), mine], buf.far.at[LOW, :, :, mine]),
        (coeffs.at[:, pl.ds(0, wide), mine], buf.far.at[HIGH, :, :, mine]),
        buf.far.at[LOW, :, :, mine], buf.far.at[HIGH, :, :, mine],
    )

    group_decay = decays()

    terms.land()
    last = members - 1
    value = buf.terms[last]
    buf.local[last] = value

    def solve(i, carry):
        value, summed = carry
        k = last - i
        value = buf.decay[k] * value + buf.terms[k]
        buf.local[k] = value
        return value, summed + jnp.where((k > 0) | (x > 0), value, 0.0)

    buf.rx_send[0], buf.rx_send[1] = lax.fori_loop(1, members, solve, (value, value), unroll=5)
    group_result = across(buf.rx_send, buf.rx)

    pair.land()

    def pair_sum(i):
        buf.d_chip[i] = buf.d[i, mine] + buf.d_pair[i]

    each(0, rows, pair_sum, rows)
    ring = along(lambda to: buf.d_chip.at[to], buf.d_ring.at[z], buf.d_ring.at[pl.ds(0, rows - 1)])
    buf.d_ring[z] = buf.d_chip[z]

    far_pair = []
    for side, exists in ((LOW, has_low), (HIGH, has_high)):
        far[side].land()
        part = buf.far.at[side, :, :, mine]
        far_pair.append(net.move(part, exists, exists).start(part, part, sibling))

    group_decay.land()
    group_result.land()
    carry = jnp.zeros((half, lanes), F32)
    e_sum = carry
    for group in reversed(range(groups)):
        buf.carry[group] = carry
        e_sum = e_sum + (buf.rx[group, 1] + buf.fx[group, 1] * carry)
        carry = buf.rx[group, 0] + buf.fx[group, 0] * carry
    e, t = buf.e, buf.t
    e[wide + z, mine] = e_sum
    e_mine = e.at[wide + z, mine]
    e_ring = along(lambda to: e_mine, e_mine, e.at[pl.ds(wide, rows - 1), mine])
    buf.t_own[...] = e_sum + carry

    carry = buf.carry[x]

    def finish(i):
        buf.back[i] = buf.local[2 * i + 1] + buf.upto[2 * i + 1] * carry

    each(0, rows, finish, 4)
    back = along(lambda to: buf.back.at[to], buf.e_own.at[z, mine], buf.e_own.at[pl.ds(0, rows - 1), mine])
    buf.e_own[z, mine] = buf.back[z]

    ring.land()
    buf.dx_send[...] = lax.fori_loop(1, rows, lambda i, s: s + buf.d_ring[i], buf.d_ring[0])
    d_across = across(buf.dx_send, buf.dx)

    e_ring.land()
    e_faces = up_down(
        (e.at[pl.ds(rows, wide), mine], e.at[rows_low, mine]), (e.at[pl.ds(wide, wide), mine], e.at[rows_high, mine]),
        e.at[rows_low, mine], e.at[rows_high, mine],
    )
    e_pair = net.move(e.at[rows_own, mine]).start(e.at[rows_own, mine], e.at[rows_own, mine], sibling)

    d_across.land()
    t_mine = buf.t_own[...]
    for group in range(groups):
        t_mine = t_mine + buf.dx[group]
    t[z, mine] = t_mine
    t_ring = along(lambda to: t.at[z, mine], t.at[z, mine], t.at[pl.ds(0, rows - 1), mine])

    def far_factors(side):
        def one(i):
            row = wide + rows + i if side == HIGH else i
            factors_x(row, buf.far[side, 0, i])
            factors_yz(row, buf.far[side, 1, i], buf.far[side, 2, i])

        each(0, wide, one, wide)

    for side, exists in ((LOW, has_low), (HIGH, has_high)):
        far_pair[side].land()
        when(exists, lambda: far_factors(side))

    e_pairs = [e_pair]
    for side, exists, where in ((LOW, has_low, rows_low), (HIGH, has_high, rows_high)):
        e_faces[side].land()
        part = e.at[where, mine]
        e_pairs.append(net.move(part, exists, exists).start(part, part, sibling))

    for pair in e_pairs:
        pair.land()

    for s in range(steps - 1):
        if s == min(3, steps - 2):
            t_ring.land()
            t_pair = net.move(t.at[:, mine]).start(t.at[:, mine], t.at[:, mine], sibling)
        if s == min(5, steps - 2):
            back.land()
            back_pair = net.move(buf.e_own.at[:, mine]).start(buf.e_own.at[:, mine], buf.e_own.at[:, mine], sibling)
        src = (e, buf.e1, buf.e2)[0 if s == 0 else 1 + (s - 1) % 2]
        dst = (buf.e1, buf.e2)[s % 2]
        reach = steps - 2 - s

        def halo_row(row, exists):
            dst[row + wide] = jnp.where(exists, stepped(src, row + wide, row), 0.0)

        def own_row(row):
            value = stepped(src, row + wide, row)
            dst[row + wide] = value
            buf.sum[row] = value if s == 0 else buf.sum[row] + value

        each(-reach, 0, lambda row: halo_row(row, has_low), rows)
        each(0, rows, own_row, rows)
        each(rows, rows + reach, lambda row: halo_row(row, has_high), rows)

    t_pair.land()
    buf.sum[...] = BETA * buf.control[...] + (t[...] + buf.sum[...]) * (1.0 / (slabs * steps))
    results = [pltpu.make_async_copy(buf.sum, gradient_out, inputs.at[0])]
    results[0].start()
    back_pair.land()

    def corrected_row(i):
        later = buf.e_own[i]
        buf.corrected[i] = guess[i] + jnp.where(core == 1, later, jnp.exp(-rate[i]) * later + buf.res[i])

    each(0, rows, corrected_row, rows)
    results.append(pltpu.make_async_copy(buf.corrected, corrected_out, inputs.at[1]))
    results[1].start()
    net.close()
    for result in results:
        result.wait()


def exchange(mesh, misfit, guess, rate, coeffs, control, rounds):
    steps, rows, mid, lanes = misfit.shape
    members, half, wide = 2 * rows, mid // 2, steps - 1
    ny = mesh.shape[SPACE]
    groups = mesh.shape[TIME] // members
    deepest = max(rounds)
    forcing_at, count = {}, 0
    for r, n in enumerate(rounds):
        for s in range(n - 1):
            forcing_at[(r, s)] = count
            count += n - 1 - s
    plane, part = (mid, lanes), (half, lanes)
    field, long, slots = (rows,) + plane, (rows + 2 * wide,) + plane, (members,) + part
    shapes = dict(
        guess=field, rate=field, control=field, corrected=field, coeffs=(3,) + field,
        cx=(2, deepest) + plane, cyz=(2, 2, max(deepest - 1, 1)) + plane,
        f_send=(2, max(count, 1)) + plane, f_halo=(2, max(count, 1)) + plane,
        rates=slots, decay=slots, upto=slots, fx_send=(2,) + part, fx=(groups, 2) + part,
        res=field, d=field, d_pair=(rows,) + part, d_chip=(rows,) + part, d_ring=(rows,) + part,
        dx_send=part, dx=(groups,) + part, t_own=part,
        terms=slots, local=slots, rx_send=(2,) + part, rx=(groups, 2) + part,
        carry=(groups,) + part, back=(rows,) + part, e_own=field, t=field, sum=field, far=(2, 3, wide) + plane,
        ax=long, bx=long, ay=long, by=long, az=long, bz=long, e=long, e1=long, e2=long,
    )
    extra = [(rows + 2 * n,) + plane for n in rounds] + [(rows + 2 * (deepest - 1),) + plane] * (deepest - 1)
    cfg = SimpleNamespace(
        names=list(shapes), steps=steps, rounds=rounds, rows=rows, mid=mid, lanes=lanes, groups=groups, ny=ny,
        forcing_at=forcing_at,
    )
    in_hbm = pl.BlockSpec(memory_space=pltpu.HBM)
    return pl.pallas_call(
        functools.partial(kernel, cfg),
        out_shape=[jax.ShapeDtypeStruct(field, F32)] * 2,
        in_specs=[in_hbm] * 5,
        out_specs=[in_hbm] * 2,
        scratch_shapes=[pltpu.VMEM(shape, F32) for shape in list(shapes.values()) + extra]
        + [pltpu.VMEM(misfit.shape, misfit.dtype), pltpu.SemaphoreType.DMA((5,))]
        + [pltpu.SemaphoreType.DMA((MAX_MOVES,))] * 2,
        compiler_params=pltpu.CompilerParams(
            collective_id=0, has_side_effects=True, vmem_limit_bytes=213 * 256 * 1024),
        name="cycle",
    )(misfit, guess, rate, coeffs, control)


def on_device(mesh, rounds, misfit, guess, rate, coeffs, control):
    corrected, gradient = exchange(mesh, misfit, guess[0], rate[0], coeffs, control, rounds)
    return corrected[None], gradient


def solution(mesh, rounds=ROUNDS):
    slab, block = P(TIME, SPACE, None, None), P(SPACE, None, None)
    return jax.shard_map(
        functools.partial(on_device, mesh, rounds),
        mesh=mesh,
        in_specs=(slab, slab, slab, P(None, SPACE, None, None), block),
        out_specs=(slab, block),
        check_vma=False,
    )
```

```python
import functools
from types import SimpleNamespace

import jax
import jax.numpy as jnp
from jax import lax
from jax.experimental import pallas as pl
from jax.experimental.pallas import tpu as pltpu
from jax.sharding import PartitionSpec as P

NU = 0.14
BETA = 0.5
CENTRE = 1.0 - 6.0 * NU
ROUNDS = (1, 2, 2, 3)
MESH = pl.DeviceIdType.MESH
F32 = jnp.float32
MAX_MOVES = 64
LOW, HIGH = 0, 1
TIME, SPACE = "tm", "space"


def rolled(value, by, axis):
    return pltpu.roll(value, by % value.shape[axis], axis)


def when(condition, run):
    def body():
        run()

    if condition is None:
        body()
    else:
        pl.when(condition)(body)


def far_first(i, count):
    return count // 2 + jnp.where(i % 2 == 0, i // 2, -(i // 2))


class Net:
    def __init__(self, send, recv, here):
        self.send, self.recv, self.here, self.moves = send, recv, here, []

    def move(self, whole, sent=None, got=None):
        return Move(self, whole, sent, got)

    def close(self):
        for move in self.moves:
            move.close()


class Move:
    def __init__(self, net, whole, sent, got):
        self.net, self.whole, self.sent, self.got = net, whole, sent, got
        self.index, self.started, self.arrived = len(net.moves), False, False
        net.moves.append(self)

    def copy(self, src, dst, device):
        return pltpu.make_async_remote_copy(
            src_ref=src, dst_ref=dst, send_sem=self.net.send.at[self.index], recv_sem=self.net.recv.at[self.index],
            device_id=device, device_id_type=MESH,
        )

    def start(self, src, dst, device):
        self.started = True
        when(self.sent, lambda: self.copy(src, dst, device).start())
        return self

    def land(self):
        self.arrived = True
        when(self.got, lambda: self.copy(self.whole, self.whole, self.net.here).wait_recv())

    def close(self):
        if self.started:
            if not self.arrived:
                self.land()
            when(self.sent, lambda: self.copy(self.whole, self.whole, self.net.here).wait_send())


def kernel(cfg, misfit_in, guess_in, rate_in, coeffs_in, control_in, corrected_out, gradient_out, *scratch):
    buf = SimpleNamespace(**dict(zip(cfg.names, scratch)))
    wf = scratch[len(cfg.names):len(cfg.names) + len(cfg.rounds)]
    mids = scratch[len(cfg.names) + len(cfg.rounds):-4]
    misfit, inputs = scratch[-4], scratch[-3]
    guess, rate, coeffs = buf.guess, buf.rate, buf.coeffs
    fetches = [
        pltpu.make_async_copy(src, dst, inputs.at[i])
        for i, (src, dst) in enumerate(((guess_in, guess), (coeffs_in, coeffs), (misfit_in, misfit), (rate_in, rate), (control_in, buf.control)))
    ]
    for fetch in fetches:
        fetch.start()
    steps, rounds, rows, mid, lanes = cfg.steps, cfg.rounds, cfg.rows, cfg.mid, cfg.lanes
    groups, ny = cfg.groups, cfg.ny
    half, members, wide = mid // 2, 2 * rows, steps - 1
    deepest = max(rounds)
    slabs = groups * members

    tm, y = lax.axis_index(TIME), lax.axis_index(SPACE)
    x, spot = tm // members, tm % members
    z, core = spot // 2, spot % 2
    base = x * members
    has_low, has_high = y > 0, y < ny - 1
    has_next, has_before = tm < slabs - 1, tm > 0
    below, above, sibling = (tm, y - 1), (tm, y + 1), (base + spot + 1 - 2 * core, y)

    net = Net(scratch[-2], scratch[-1], (tm, y))
    ax, bx, ay, by, az, bz = buf.ax, buf.bx, buf.ay, buf.by, buf.az, buf.bz
    mine = pl.ds(pl.multiple_of(core * half, half), half)
    other = pl.ds(pl.multiple_of((1 - core) * half, half), half)
    rows_own, rows_low, rows_high = pl.ds(wide, rows), pl.ds(0, wide), pl.ds(wide + rows, wide)

    barrier = pltpu.get_barrier_semaphore()

    def greet(device):
        pl.semaphore_signal(barrier, inc=1, device_id=device, device_id_type=MESH)

    def greet_member(i, _):
        greet((base + (spot + far_first(i, members)) % members, y))
        return 0

    lax.fori_loop(1, members, greet_member, 0, unroll=members - 1)
    for i in range(1, groups):
        greet(((x + i) % groups * members + spot, y))
    when(has_low, lambda: greet(below))
    when(has_high, lambda: greet(above))
    for exists, there in ((has_next, tm + 1), (has_before, tm - 1)):
        when(exists, lambda: greet((there, y)))
        when(exists & has_low, lambda: greet((there, y - 1)))
        when(exists & has_high, lambda: greet((there, y + 1)))
    sides = has_low.astype(jnp.int32) + has_high.astype(jnp.int32)
    ends = has_next.astype(jnp.int32) + has_before.astype(jnp.int32)

    for fetch in fetches:
        fetch.wait()
    for r, n in enumerate(rounds):
        for s in range(n - 1):
            k, turn, width = cfg.forcing_at[(r, s)], sum(rounds[:r]) + s, n - 1 - s
            for i in range(width):
                buf.f_send[LOW, k + i] = misfit[steps - 1 - turn, rows - width + i].astype(F32)
                buf.f_send[HIGH, k + i] = misfit[steps - 1 - turn, i].astype(F32)

    pl.semaphore_wait(barrier, members - 1 + groups - 1 + sides + ends + sides * ends)

    first = rounds[0]
    start = net.move(wf[0].at[pl.ds(first, rows)], has_before, has_next)
    start.start(guess, wf[0].at[pl.ds(first, rows)], (tm - 1, y))

    def up_down(low, high, whole_low, whole_high):
        up = net.move(whole_low, has_high, has_low)
        down = net.move(whole_high, has_low, has_high)
        up.start(low[0], low[1], above)
        down.start(high[0], high[1], below)
        return up, down

    lows, highs = wf[0].at[pl.ds(0, first)], wf[0].at[pl.ds(first + rows, first)]
    start_up = net.move(lows, has_before & has_high, has_next & has_low)
    start_up.start(guess.at[pl.ds(rows - first, first)], lows, (tm - 1, y + 1))
    start_down = net.move(highs, has_before & has_low, has_next & has_high)
    start_down.start(guess.at[pl.ds(0, first)], highs, (tm - 1, y - 1))
    start_faces = (start_up, start_down)

    def both_ends(src, at_low, at_high, dst):
        return up_down((src.at[at_high], dst.at[LOW]), (src.at[at_low], dst.at[HIGH]), dst.at[LOW], dst.at[HIGH])

    def ends(src, at, width, low_halo, high_halo, depth):
        up, down = low_halo.at[pl.ds(depth - at - width, width)], high_halo.at[pl.ds(at, width)]
        return up_down((src.at[pl.ds(rows - at - width, width)], up), (src.at[pl.ds(at, width)], down), up, down)

    def reach_of(r):
        before = max((0,) + rounds[:r])
        after = max(before, rounds[r])
        return before, after, max(before - 1, 0), after - 1

    def near_stage(r):
        before, after, yz_before, yz_after = reach_of(r)
        moves = []
        if after > before:
            moves.append(ends(coeffs.at[0], before, after - before, buf.cx.at[LOW], buf.cx.at[HIGH], deepest))
        if yz_after > yz_before:
            for i in range(2):
                moves.append(ends(coeffs.at[1 + i], yz_before, yz_after - yz_before, buf.cyz.at[LOW, i], buf.cyz.at[HIGH, i],
                                  deepest - 1))
        n = rounds[r]
        if n > 1:
            part = pl.ds(cfg.forcing_at[(r, 0)], n * (n - 1) // 2)
            low, high = buf.f_halo.at[LOW, part], buf.f_halo.at[HIGH, part]
            moves.append(up_down((buf.f_send.at[LOW, part], low), (buf.f_send.at[HIGH, part], high), low, high))
        return moves

    near = [near_stage(r) for r in range(min(2, len(rounds)))]

    def transpose(src, dst):
        move = net.move(dst.at[pl.ds(0, members - 1)])

        def send(i, _):
            to = (spot + far_first(i, members)) % members
            part = src.at[to // 2, pl.ds(pl.multiple_of(to % 2 * half, half), half)]
            move.start(part, dst.at[spot], (base + to, y))
            return 0

        lax.fori_loop(1, members, send, 0, unroll=members - 1)
        dst[spot] = src[z, mine]
        return move

    def across(src, dst):
        move = net.move(dst.at[pl.ds(0, groups - 1)])
        for i in sorted(range(1, groups), key=lambda i: -min(i, groups - i)):
            move.start(src, dst.at[x], ((x + i) % groups * members + spot, y))
        dst[x] = src[...]
        return move

    def along(source, target, whole):
        move = net.move(whole)

        def send(i, _):
            to = (z + far_first(i, rows)) % rows
            move.start(source(to), target, (base + 2 * to + core, y))
            return 0

        lax.fori_loop(1, rows, send, 0, unroll=rows - 1)
        return move

    def factors_x(row, c):
        ax[row] = NU + 0.5 * c
        bx[row] = NU - 0.5 * c

    def factors_yz(row, cy, cz):
        place = lax.broadcasted_iota(jnp.int32, (mid, lanes), 0)
        ay[row] = jnp.where(place == 0, 0.0, NU + 0.5 * cy)
        by[row] = jnp.where(place == mid - 1, 0.0, NU - 0.5 * cy)
        place = lax.broadcasted_iota(jnp.int32, (mid, lanes), 1)
        az[row] = jnp.where(place == 0, 0.0, NU + 0.5 * cz)
        bz[row] = jnp.where(place == lanes - 1, 0.0, NU - 0.5 * cz)

    def each(start, stop, run, unroll=1):
        def one(i, _):
            run(i)
            return 0

        if stop > start:
            lax.fori_loop(start, stop, one, 0, unroll=min(unroll, stop - start))

    def own_factors(i):
        factors_x(wide + i, coeffs[0, i])
        factors_yz(wide + i, coeffs[1, i], coeffs[2, i])

    each(0, rows, own_factors, 4)

    def clear(ref, start, count):
        def one(i):
            ref[i] = jnp.zeros((mid, lanes), F32)

        each(start, start + count, one)

    halos = [(ref, n) for ref, n in zip(wf[1:], rounds[1:])] + [(buf.e, wide), (buf.e1, wide), (buf.e2, wide)]

    @pl.when(jnp.logical_not(has_low))
    def _():
        clear(bx, 0, wide)
        for ref, n in halos:
            clear(ref, 0, n)

    @pl.when(jnp.logical_not(has_high))
    def _():
        clear(ax, wide + rows, wide)
        for ref, n in halos:
            clear(ref, n + rows, n)

    when(jnp.logical_not(has_next & has_low), lambda: clear(wf[0], 0, first))
    when(jnp.logical_not(has_next & has_high), lambda: clear(wf[0], first + rows, first))
    when(jnp.logical_not(has_next), lambda: clear(wf[0], first, rows))

    def stepped(src, at, row):
        w = src[at]
        place = row + wide
        value = CENTRE * w
        value = value + (ax[place + 1] * src[at + 1] + bx[place - 1] * src[at - 1])
        value = value + (rolled(ay[place] * w, -1, 0) + rolled(by[place] * w, 1, 0))
        return value + (rolled(az[place] * w, -1, 1) + rolled(bz[place] * w, 1, 1))

    def relax_row(r, s, row, side=None):
        n = rounds[r]
        turn = sum(rounds[:r]) + s
        src, shift = (wf[r], n) if s == 0 else (mids[s - 1], deepest - 1)
        if side is None:
            forcing = misfit[steps - 1 - turn, row].astype(F32)
        elif side == LOW:
            forcing = buf.f_halo[LOW, cfg.forcing_at[(r, s)] + (n - 1 - s) + row]
        else:
            forcing = buf.f_halo[HIGH, cfg.forcing_at[(r, s)] + row - rows]
        value = stepped(src, row + shift, row) + forcing
        if side is not None:
            value = jnp.where(has_low if side == LOW else has_high, value, 0.0)
        if s < n - 1:
            mids[s][row + deepest - 1] = value
        elif r < len(rounds) - 1:
            wf[r + 1][row + rounds[r + 1]] = value
        if side is None:
            if turn == 0:
                buf.d[row] = guess[row] + value
            elif turn < steps - 1:
                buf.d[row] = buf.d[row] + value
            else:
                buf.res[row] = value - guess[row]

    def inner(r):
        for s in range(rounds[r]):
            each(s + 1, rows - 1 - s, lambda row: relax_row(r, s, row), rows)

    def outer(r):
        for s in range(rounds[r]):
            reach = rounds[r] - 1 - s
            for i in range(reach):
                relax_row(r, s, -1 - i, LOW)
                relax_row(r, s, rows + i, HIGH)
            for i in range(s + 1):
                relax_row(r, s, i)
                relax_row(r, s, rows - 1 - i)

    def near_factors(r, side):
        before, after, yz_before, yz_after = reach_of(r)
        for k in range(before, after):
            if side == HIGH:
                factors_x(wide + rows + k, buf.cx[HIGH, k])
            else:
                factors_x(wide - 1 - k, buf.cx[LOW, deepest - 1 - k])
        for k in range(yz_before, yz_after):
            if side == HIGH:
                factors_yz(wide + rows + k, buf.cyz[HIGH, 0, k], buf.cyz[HIGH, 1, k])
            else:
                factors_yz(wide - 1 - k, buf.cyz[LOW, 0, deepest - 2 - k], buf.cyz[LOW, 1, deepest - 2 - k])

    def decays():
        rates.land()
        last = members - 1
        factor = jnp.exp(-buf.rates[last])
        buf.decay[last] = factor
        buf.upto[last] = factor

        def one(i, carry):
            upto, summed = carry
            k = last - i
            factor = jnp.exp(-buf.rates[k])
            upto = factor * upto
            buf.decay[k] = factor
            buf.upto[k] = upto
            return upto, summed + jnp.where((k > 0) | (x > 0), upto, 0.0)

        buf.fx_send[0], buf.fx_send[1] = lax.fori_loop(1, members, one, (factor, factor), unroll=3)
        return across(buf.fx_send, buf.fx)

    start.land()
    faces = start_faces
    for r in range(len(rounds)):
        inner(r)
        if r < len(rounds) - 1:
            n, ref = rounds[r + 1], wf[r + 1]
            low, high = ref.at[pl.ds(0, n)], ref.at[pl.ds(n + rows, n)]
            coming = net.move(low, has_high, has_low), net.move(high, has_low, has_high)
        for side, exists in ((LOW, has_low), (HIGH, has_high)):
            for pair in near[r]:
                pair[side].land()
            if near[r]:
                when(exists, lambda: near_factors(r, side))
            faces[side].land()
        outer(r)
        if r < len(rounds) - 1:
            coming[HIGH].start(ref.at[pl.ds(n, n)], high, below)
            coming[LOW].start(ref.at[pl.ds(rows, n)], low, above)
            if r + 2 < len(rounds):
                near.append(near_stage(r + 2))
        if r == 0:
            rates = transpose(rate, buf.rates)
        if r < len(rounds) - 1:
            faces = coming

    terms = transpose(buf.res, buf.terms)
    pair = net.move(buf.d_pair).start(buf.d.at[:, other], buf.d_pair, sibling)
    far = up_down(
        (coeffs.at[:, pl.ds(rows - wide, wide), mine], buf.far.at[LOW, :, :, mine]),
        (coeffs.at[:, pl.ds(0, wide), mine], buf.far.at[HIGH, :, :, mine]),
        buf.far.at[LOW, :, :, mine], buf.far.at[HIGH, :, :, mine],
    )

    group_decay = decays()

    terms.land()
    last = members - 1
    value = buf.terms[last]
    buf.local[last] = value

    def solve(i, carry):
        value, summed = carry
        k = last - i
        value = buf.decay[k] * value + buf.terms[k]
        buf.local[k] = value
        return value, summed + jnp.where((k > 0) | (x > 0), value, 0.0)

    buf.rx_send[0], buf.rx_send[1] = lax.fori_loop(1, members, solve, (value, value), unroll=members - 1)
    group_result = across(buf.rx_send, buf.rx)

    pair.land()

    def pair_sum(i):
        buf.d_chip[i] = buf.d[i, mine] + buf.d_pair[i]

    each(0, rows, pair_sum, rows)
    ring = along(lambda to: buf.d_chip.at[to], buf.d_ring.at[z], buf.d_ring.at[pl.ds(0, rows - 1)])
    buf.d_ring[z] = buf.d_chip[z]

    far_pair = []
    for side, exists in ((LOW, has_low), (HIGH, has_high)):
        far[side].land()
        part = buf.far.at[side, :, :, mine]
        far_pair.append(net.move(part, exists, exists).start(part, part, sibling))

    group_decay.land()
    group_result.land()
    carry = jnp.zeros((half, lanes), F32)
    e_sum = carry
    for group in reversed(range(groups)):
        buf.carry[group] = carry
        e_sum = e_sum + (buf.rx[group, 1] + buf.fx[group, 1] * carry)
        carry = buf.rx[group, 0] + buf.fx[group, 0] * carry
    e, t = buf.e, buf.t
    e[wide + z, mine] = e_sum
    e_mine = e.at[wide + z, mine]
    e_ring = along(lambda to: e_mine, e_mine, e.at[pl.ds(wide, rows - 1), mine])
    buf.t_own[...] = e_sum + carry

    carry = buf.carry[x]

    def finish(i):
        buf.back[i] = buf.local[2 * i + 1] + buf.upto[2 * i + 1] * carry

    each(0, rows, finish, 4)
    back = along(lambda to: buf.back.at[to], buf.e_own.at[z, mine], buf.e_own.at[pl.ds(0, rows - 1), mine])
    buf.e_own[z, mine] = buf.back[z]

    ring.land()
    buf.dx_send[...] = lax.fori_loop(1, rows, lambda i, s: s + buf.d_ring[i], buf.d_ring[0])
    d_across = across(buf.dx_send, buf.dx)

    e_ring.land()
    e_faces = up_down(
        (e.at[pl.ds(rows, wide), mine], e.at[rows_low, mine]), (e.at[pl.ds(wide, wide), mine], e.at[rows_high, mine]),
        e.at[rows_low, mine], e.at[rows_high, mine],
    )
    e_pair = net.move(e.at[rows_own, mine]).start(e.at[rows_own, mine], e.at[rows_own, mine], sibling)

    d_across.land()
    t_mine = buf.t_own[...]
    for group in range(groups):
        t_mine = t_mine + buf.dx[group]
    t[z, mine] = t_mine
    t_ring = along(lambda to: t.at[z, mine], t.at[z, mine], t.at[pl.ds(0, rows - 1), mine])

    def far_factors(side):
        def one(i):
            row = wide + rows + i if side == HIGH else i
            factors_x(row, buf.far[side, 0, i])
            factors_yz(row, buf.far[side, 1, i], buf.far[side, 2, i])

        each(0, wide, one, wide)

    for side, exists in ((LOW, has_low), (HIGH, has_high)):
        far_pair[side].land()
        when(exists, lambda: far_factors(side))

    e_pairs = [e_pair]
    for side, exists, where in ((LOW, has_low, rows_low), (HIGH, has_high, rows_high)):
        e_faces[side].land()
        part = e.at[where, mine]
        e_pairs.append(net.move(part, exists, exists).start(part, part, sibling))

    for pair in e_pairs:
        pair.land()

    for s in range(steps - 1):
        if s == min(3, steps - 2):
            t_ring.land()
            t_pair = net.move(t.at[:, mine]).start(t.at[:, mine], t.at[:, mine], sibling)
        if s == min(5, steps - 2):
            back.land()
            back_pair = net.move(buf.e_own.at[:, mine]).start(buf.e_own.at[:, mine], buf.e_own.at[:, mine], sibling)
        src = (e, buf.e1, buf.e2)[0 if s == 0 else 1 + (s - 1) % 2]
        dst = (buf.e1, buf.e2)[s % 2]
        reach = steps - 2 - s

        def halo_row(row, exists):
            dst[row + wide] = jnp.where(exists, stepped(src, row + wide, row), 0.0)

        def own_row(row):
            value = stepped(src, row + wide, row)
            dst[row + wide] = value
            buf.sum[row] = value if s == 0 else buf.sum[row] + value

        each(-reach, 0, lambda row: halo_row(row, has_low), rows)
        each(0, rows, own_row, rows)
        each(rows, rows + reach, lambda row: halo_row(row, has_high), rows)

    t_pair.land()
    buf.sum[...] = BETA * buf.control[...] + (t[...] + buf.sum[...]) * (1.0 / (slabs * steps))
    results = [pltpu.make_async_copy(buf.sum, gradient_out, inputs.at[0])]
    results[0].start()
    back_pair.land()

    def corrected_row(i):
        later = buf.e_own[i]
        buf.corrected[i] = guess[i] + jnp.where(core == 1, later, jnp.exp(-rate[i]) * later + buf.res[i])

    each(0, rows, corrected_row, rows)
    results.append(pltpu.make_async_copy(buf.corrected, corrected_out, inputs.at[1]))
    results[1].start()
    net.close()
    for result in results:
        result.wait()


def exchange(mesh, misfit, guess, rate, coeffs, control, rounds):
    steps, rows, mid, lanes = misfit.shape
    members, half, wide = 2 * rows, mid // 2, steps - 1
    ny = mesh.shape[SPACE]
    groups = mesh.shape[TIME] // members
    deepest = max(rounds)
    forcing_at, count = {}, 0
    for r, n in enumerate(rounds):
        for s in range(n - 1):
            forcing_at[(r, s)] = count
            count += n - 1 - s
    plane, part = (mid, lanes), (half, lanes)
    field, long, slots = (rows,) + plane, (rows + 2 * wide,) + plane, (members,) + part
    shapes = dict(
        guess=field, rate=field, control=field, corrected=field, coeffs=(3,) + field,
        cx=(2, deepest) + plane, cyz=(2, 2, max(deepest - 1, 1)) + plane,
        f_send=(2, max(count, 1)) + plane, f_halo=(2, max(count, 1)) + plane,
        rates=slots, decay=slots, upto=slots, fx_send=(2,) + part, fx=(groups, 2) + part,
        res=field, d=field, d_pair=(rows,) + part, d_chip=(rows,) + part, d_ring=(rows,) + part,
        dx_send=part, dx=(groups,) + part, t_own=part,
        terms=slots, local=slots, rx_send=(2,) + part, rx=(groups, 2) + part,
        carry=(groups,) + part, back=(rows,) + part, e_own=field, t=field, sum=field, far=(2, 3, wide) + plane,
        ax=long, bx=long, ay=long, by=long, az=long, bz=long, e=long, e1=long, e2=long,
    )
    extra = [(rows + 2 * n,) + plane for n in rounds] + [(rows + 2 * (deepest - 1),) + plane] * (deepest - 1)
    cfg = SimpleNamespace(
        names=list(shapes), steps=steps, rounds=rounds, rows=rows, mid=mid, lanes=lanes, groups=groups, ny=ny,
        forcing_at=forcing_at,
    )
    in_hbm = pl.BlockSpec(memory_space=pltpu.HBM)
    return pl.pallas_call(
        functools.partial(kernel, cfg),
        out_shape=[jax.ShapeDtypeStruct(field, F32)] * 2,
        in_specs=[in_hbm] * 5,
        out_specs=[in_hbm] * 2,
        scratch_shapes=[pltpu.VMEM(shape, F32) for shape in list(shapes.values()) + extra]
        + [pltpu.VMEM(misfit.shape, misfit.dtype), pltpu.SemaphoreType.DMA((5,))]
        + [pltpu.SemaphoreType.DMA((MAX_MOVES,))] * 2,
        compiler_params=pltpu.CompilerParams(
            collective_id=0, has_side_effects=True, vmem_limit_bytes=213 * 256 * 1024),
        name="cycle",
    )(misfit, guess, rate, coeffs, control)


def on_device(mesh, rounds, misfit, guess, rate, coeffs, control):
    corrected, gradient = exchange(mesh, misfit, guess[0], rate[0], coeffs, control, rounds)
    return corrected[None], gradient


def solution(mesh, rounds=ROUNDS):
    slab, block = P(TIME, SPACE, None, None), P(SPACE, None, None)
    return jax.shard_map(
        functools.partial(on_device, mesh, rounds),
        mesh=mesh,
        in_specs=(slab, slab, slab, P(None, SPACE, None, None), block),
        out_specs=(slab, block),
        check_vma=False,
    )
```
